128 devices in a mesh: row: 8 (over z, core), col: 16 (over y, x).
Axes of the slice: x: 4, y: 4, z: 4, core: 2. Of those that a mesh axis runs over, the one named last changes fastest.
Arguments:
- tile_values: bfloat16 [8, 384, 128, 128], P('row', 'col'), may hold values from -0.5 to 0.5
- tile_rows: int32 [8, 384], P('row', 'col'), may hold values from 0 to 47, as said below
Outputs:
- expanded: bfloat16 [8, 8, 384, 128, 128], P('row', None, 'col')
The draws below stay inside these ranges and needn't reach their ends.
Inputs may be any that keep to these rules, and one draw needn't show every extreme that they name: For each row panel p and each aligned run of 24 block columns, the entries tile_rows[p, run] take exactly 8 distinct values, all inside one aligned run of 24 block rows of the panel.
All inputs are finite; a program needn't handle non-finite values.
Results may differ from the reference program's by a relative error of at most 0.001.
Values may be sent and summed in bfloat16 or wider, within the bound.
No kernel may reach another device: no remote copies, remote signals or barrier semaphores. Data moves between devices by JAX's collectives and lax.ppermute only.
A program may use at most 64 MiB of HBM per device.

```python
import jax
import jax.numpy as jnp
from jax import lax

TILE = 128
BLK = 24
USED = 8
PANELS = 8
NB = 384
BRD = 48


def draw_tile_rows(key, part):
    key = jax.random.fold_in(key, 7)
    col_count = NB // BLK
    runs = BRD // BLK
    groups = PANELS * col_count
    hub_key, first_key, second_key, pick_key = jax.random.split(key, 4)
    hub_order = jax.random.permutation(hub_key, runs)
    first = jax.random.randint(first_key, (groups,), 0, runs)
    second = jax.random.randint(second_key, (groups,), 0, runs)
    chosen_run = hub_order[first * second // runs]
    chosen_run = chosen_run.at[0].set(runs - 1).at[groups - 1].set(0)
    edge_rows = jnp.full((groups,), -1, dtype=jnp.int32)
    edge_rows = edge_rows.at[0].set(BLK - 1).at[groups - 1].set(0)

    def one_group(group_key, run_start, edge):
        pick_part, fill_part, order_part = jax.random.split(group_key, 3)
        distinct_rows = jax.random.permutation(pick_part, BLK)[:USED].astype(jnp.int32)
        present = jnp.any(distinct_rows == edge)
        forced = distinct_rows.at[0].set(edge)
        distinct_rows = jnp.where((edge >= 0) & jnp.logical_not(present), forced, distinct_rows)
        extra = jax.random.randint(fill_part, (BLK - USED,), 0, USED)
        slots = jnp.concatenate([jnp.arange(USED, dtype=jnp.int32), extra.astype(jnp.int32)])
        slots = jax.random.permutation(order_part, slots)
        return (run_start * BLK + distinct_rows[slots]).astype(jnp.int32)
    group_keys = jax.random.split(pick_key, groups)
    rows = jax.vmap(one_group)(group_keys, chosen_run, edge_rows)
    return rows.reshape(PANELS, NB).astype(jnp.int32)


def steps_of(key, extent, pieces, low, high):
    gain = 1.0
    for axis_at, parts in pieces:
        steps = jax.random.uniform(jax.random.fold_in(jax.random.fold_in(key, 6), axis_at), (parts,), jnp.float32, low / len(pieces), high / len(pieces))
        gain = gain * jnp.repeat(jnp.exp(steps), extent[axis_at] // parts).reshape((-1,) + (1,) * (len(extent) - 1 - axis_at))
    return gain


def noise(own_key, shape, deviation, limit, shards=(), held_as=jnp.bfloat16):
    factor_of = steps_of(own_key, shape, shards, -0.22, 0.18) if shards else 1.0
    entries = jax.random.normal(own_key, shape, jnp.float32) * deviation * factor_of
    return jnp.minimum(jnp.maximum(entries, -limit), limit).astype(held_as)


def setup_inputs(seed: int = 0) -> dict:
    seeds = jax.random.split(jax.random.key(seed), 3)
    return {
        "tile_values": noise(seeds[0], (PANELS, NB, TILE, TILE), TILE ** -0.5, 0.5, ((0, 8), (1, 16))),
        "tile_rows": draw_tile_rows(jax.random.fold_in(seeds[2], 71), 0),
    }


def reference(tile_values, tile_rows):
    panels = tile_values.shape[0]
    total_cols = tile_values.shape[1]
    panel_rows = total_cols // panels
    tile_size = tile_values.shape[2]
    inner_index = (jnp.arange(panels, dtype=jnp.int32)[:, None] * panel_rows + tile_rows).astype(jnp.int32)
    lower = (jnp.arange(panels)[None, :] < jnp.arange(panels)[:, None])
    right_tiles = tile_values.astype(jnp.float32)

    def one_panel(panel_pair):
        panel_vals, panel_tile_rows = panel_pair
        left_tiles = panel_vals[inner_index].astype(jnp.float32)
        out_rows = panel_tile_rows[inner_index]
        products = jnp.einsum('qcab,qcbd->qcad', left_tiles, right_tiles, precision=lax.Precision.HIGHEST)
        matches = out_rows[:, None, :] == out_rows[None, :, :]
        merged = jnp.einsum('qsc,scab->qcab', matches.astype(jnp.float32), products, precision=lax.Precision.HIGHEST)
        inflated = merged * merged
        repeated = jnp.any(matches & lower[:, :, None], axis=1)
        first_mask = 1.0 - repeated.astype(jnp.float32)
        partial_sums = jnp.einsum('qc,qcab->cb', first_mask, inflated, precision=lax.Precision.HIGHEST)
        return inflated, partial_sums

    inflated, partial_sums = lax.map(one_panel, (tile_values, tile_rows))
    column_total = jnp.sum(partial_sums, axis=0)
    scaling = float(panels * panels * tile_size)
    factor = scaling / (column_total + 1e-6)
    return (inflated * factor[None, None, :, None, :]).astype(jnp.bfloat16)
```

```python
import jax
import jax.numpy as jnp
import numpy as np
from jax import lax
from jax.experimental import pallas as pl
from jax.experimental.pallas import tpu as pltpu
from jax.sharding import Mesh, PartitionSpec as P

TILE = 128
BLK = 24
USED = 8
PANELS = 8
COLS = 16
BRD = 48
HALF = BLK // 2
DZ = (0, 3, 1, 2)
INNER = [(0, 1), (1, 0), (2, 3), (3, 2)]
OUTER = [(0, 3), (3, 0), (1, 2), (2, 1)]
UP = [(i, (i + 1) % 4) for i in range(4)]
DOWN = [(i, (i + 3) % 4) for i in range(4)]
SWAP = [(0, 1), (1, 0)]

SMEM = pl.BlockSpec(memory_space=pltpu.SMEM)
VMEM = pl.BlockSpec(memory_space=pltpu.VMEM)


def zero_table(ref, size):
    def step(n, carry):
        ref[n] = jnp.int32(-1)
        return carry

    lax.fori_loop(0, size, step, 0)


def copy_used(meta, seen, place, panel, column, first_half, put):
    zero_table(seen, BRD)

    def step(t, count):
        row = meta[column, panel * BLK + t]
        fresh = seen[row] < 0
        upper = (row >= BLK).astype(jnp.int32)
        local = row - upper * BLK

        @pl.when(fresh)
        def _():
            seen[row] = count
            put(count, upper, local)

        return count + fresh.astype(jnp.int32)

    lax.fori_loop(0, BLK, step, jnp.int32(0))


def select_own_kernel(pos, meta, own, inner, out, seen):
    x, y = pos[0], pos[1]
    panel = 2 * y + x // 2
    side = x % 2
    for dest in range(4):

        def put(slot, upper, local, dest=dest):
            @pl.when(upper == side)
            def _():
                out[dest, slot] = own[local]

            @pl.when(upper != side)
            def _():
                out[dest, slot] = inner[local]

        copy_used(meta, seen, None, panel, dest * 4 + x, None, put)


def select_other_kernel(pos, meta, outer, diag_a, diag_b, out, seen):
    x, y = pos[0], pos[1]
    panel = 2 * y + 1 - x // 2
    side = (3 - x) % 2
    for dest in range(4):

        def put(slot, upper, local, dest=dest):
            @pl.when(upper == side)
            def _():
                out[dest, slot] = outer[local]

            @pl.when((upper != side) & (local < HALF))
            def _():
                out[dest, slot] = diag_a[local]

            @pl.when((upper != side) & (local >= HALF))
            def _():
                out[dest, slot] = diag_b[local - HALF]

        copy_used(meta, seen, None, panel, dest * 4 + x, None, put)


def select(kernel, pos, meta, *blocks):
    return pl.pallas_call(
        kernel,
        out_shape=jax.ShapeDtypeStruct((4, USED, TILE, TILE), jnp.bfloat16),
        in_specs=[SMEM, SMEM] + [VMEM] * len(blocks),
        out_specs=VMEM,
        scratch_shapes=[pltpu.SMEM((BRD,), jnp.int32)],
        compiler_params=pltpu.CompilerParams(vmem_limit_bytes=16 << 20),
        cost_estimate=pl.CostEstimate(flops=0, bytes_accessed=4 << 20, transcendentals=0),
    )(pos, meta, *blocks)


def panel_of(pos, j):
    z = (pos[2] + DZ[j % 4]) % 4
    core = pos[3] if j < 4 else 1 - pos[3]
    return z, 2 * z + core


def plan_kernel(pos, meta, slot, rep, seen, stamp):
    column = pos[1] * 4 + pos[0]
    mine = 2 * pos[2] + pos[3]
    zero_table(seen, PANELS * BRD)
    zero_table(stamp, BRD)

    def step(t, counts):
        later = []
        for j in range(PANELS):
            _, panel = panel_of(pos, j)
            row = meta[column, panel * BLK + t]
            upper = (row >= BLK).astype(jnp.int32)
            old = seen[j * BRD + row]
            fresh = old < 0
            place = jnp.where(fresh, counts[j], old)
            seen[j * BRD + row] = place
            slot[j * BLK + t] = place
            later.append(counts[j] + fresh.astype(jnp.int32))
            out_row = meta[2 * panel + upper, mine * BLK + row - upper * BLK]
            mark = stamp[out_row]
            now = jnp.where(mark >= t * PANELS, mark, t * PANELS + j)
            stamp[out_row] = now
            rep[j * BLK + t] = now - t * PANELS
        return tuple(later)

    lax.fori_loop(0, BLK, step, (jnp.int32(0),) * PANELS)


def make_plan(pos, meta):
    shape = jax.ShapeDtypeStruct((PANELS * BLK,), jnp.int32)
    return pl.pallas_call(
        plan_kernel,
        out_shape=(shape, shape),
        in_specs=[SMEM, SMEM],
        out_specs=(SMEM, SMEM),
        scratch_shapes=[pltpu.SMEM((PANELS * BRD,), jnp.int32), pltpu.SMEM((BRD,), jnp.int32)],
        cost_estimate=pl.CostEstimate(flops=0, bytes_accessed=4 << 20, transcendentals=0),
    )(pos, meta)


def main_kernel(pos, slot, rep, left1, left2, *refs):
    mine, theirs, (merged, totals) = refs[:5], refs[5:10], refs[10:]

    def work(first_left, second_left):
        for half in range(2):

            def step(n, carry, half=half):
                t = half * HALF + n
                for j in range(PANELS):
                    lefts, rights = (first_left, mine) if j < 4 else (second_left, theirs)
                    d = j % 4
                    z, _ = panel_of(pos, j)
                    right = rights[d][t] if d < 3 else rights[3 + half][n]
                    product = jnp.dot(lefts[z, slot[j * BLK + t]], right, preferred_element_type=jnp.float32)
                    if j == 0:
                        merged[t, 0] = product
                    else:
                        r = rep[j * BLK + t]
                        merged[t, r] = jnp.where(r == j, 0.0, merged[t, r]) + product
                total = jnp.zeros((8, TILE), jnp.float32)
                for j in range(PANELS):
                    tile = merged[t, j]
                    part = jnp.sum((tile * tile).reshape(16, 8, TILE), axis=0)
                    total = total + jnp.where(rep[j * BLK + t] == j, part, 0.0)
                total = jnp.sum(total, axis=0, keepdims=True)
                for i in range(PANELS):
                    totals[i, pl.ds(t, 1), :] = total
                return carry

            lax.fori_loop(0, HALF, step, 0)

    own_is_mine = pos[0] // 2 == pos[3]

    @pl.when(own_is_mine)
    def _():
        work(left1, left2)

    @pl.when(jnp.logical_not(own_is_mine))
    def _():
        work(left2, left1)


def multiply(pos, slot, rep, left1, left2, mine, theirs):
    return pl.pallas_call(
        main_kernel,
        out_shape=(
            jax.ShapeDtypeStruct((BLK, PANELS, TILE, TILE), jnp.float32),
            jax.ShapeDtypeStruct((PANELS, BLK, TILE), jnp.float32),
        ),
        in_specs=[SMEM] * 3 + [VMEM] * 12,
        out_specs=(VMEM, VMEM),
        compiler_params=pltpu.CompilerParams(vmem_limit_bytes=40 << 20),
        cost_estimate=pl.CostEstimate(flops=2 * 192 * TILE**3, bytes_accessed=20 << 20, transcendentals=0),
    )(pos, slot, rep, left1, left2, *mine, *theirs)


def scale_kernel(pos, rep, merged, totals, out, factor):
    j = pl.program_id(0)

    @pl.when(j == 0)
    def _():
        factor[...] = float(PANELS * PANELS * TILE) / (jnp.sum(totals[...], axis=0) + 1e-6)

    def step(t, carry):
        tile = merged[t, rep[j * BLK + t]]
        out[0, t] = (tile * tile * factor[pl.ds(t, 1), :]).astype(jnp.bfloat16)
        return carry

    lax.fori_loop(0, BLK, step, 0)


def scale(pos, rep, merged, totals):
    def place(j, pos, rep):
        dz = jnp.where(j % 4 == 1, 3, jnp.where(j % 4 == 2, 1, jnp.where(j % 4 == 3, 2, 0)))
        core = jnp.where(j < 4, pos[3], 1 - pos[3])
        return 2 * ((pos[2] + dz) % 4) + core, 0, 0, 0

    return pl.pallas_call(
        scale_kernel,
        out_shape=jax.ShapeDtypeStruct((PANELS, BLK, TILE, TILE), jnp.bfloat16),
        grid_spec=pltpu.PrefetchScalarGridSpec(
            num_scalar_prefetch=2,
            grid=(PANELS,),
            in_specs=[VMEM, VMEM],
            out_specs=pl.BlockSpec((1, BLK, TILE, TILE), place),
            scratch_shapes=[pltpu.VMEM((BLK, TILE), jnp.float32)],
        ),
        compiler_params=pltpu.CompilerParams(vmem_limit_bytes=24 << 20),
        cost_estimate=pl.CostEstimate(flops=2 * 192 * TILE**2, bytes_accessed=20 << 20, transcendentals=0),
    )(pos, rep, merged, totals)


def on_device(tile_values, tile_rows):
    own = tile_values[0]
    pos = jnp.stack([lax.axis_index(a) for a in ("x", "y", "z", "core")]).astype(jnp.int32)

    inner = lax.ppermute(own, "x", INNER)
    outer = lax.ppermute(own, "x", OUTER)
    below = lax.ppermute(own, "z", UP)
    above = lax.ppermute(own, "z", DOWN)

    rows = lax.all_to_all(jnp.broadcast_to(tile_rows, (PANELS, BLK)), ("z", "core"), 0, 0)
    meta = lax.all_to_all(
        jnp.broadcast_to(rows.reshape(1, PANELS * BLK), (COLS, PANELS * BLK)), ("y", "x"), 0, 0
    )

    diag_a = lax.ppermute(outer[:HALF], "x", INNER)
    diag_b = lax.ppermute(inner[HALF:], "x", OUTER)
    far_a = lax.ppermute(below[:HALF], "z", UP)
    far_b = lax.ppermute(above[HALF:], "z", DOWN)

    send1 = select(select_own_kernel, pos, meta, own, inner)
    left1 = lax.all_to_all(send1, "y", 0, 0)
    send2 = select(select_other_kernel, pos, meta, outer, diag_a, diag_b)
    left2 = lax.all_to_all(send2, "y", 0, 0)

    mine = (own, below, above, far_a, far_b)
    theirs = tuple(lax.ppermute(block, "core", SWAP) for block in mine)
    slot, rep = make_plan(pos, meta)
    merged, totals = multiply(pos, slot, rep, left1, left2, mine, theirs)
    totals = lax.all_to_all(totals, ("z", "core"), 0, 0)
    return scale(pos, rep, merged, totals)[None]


def solution(mesh):
    fine = Mesh(np.asarray(mesh.devices).reshape(4, 2, 4, 4), ("z", "core", "y", "x"))
    rows, cols = ("z", "core"), ("y", "x")
    return jax.shard_map(
        on_device,
        mesh=fine,
        in_specs=(P(rows, cols, None, None), P(rows, cols)),
        out_specs=P(rows, None, cols, None, None),
        check_vma=False,
    )
```

```python
import jax
import jax.numpy as jnp
import numpy as np
from jax import lax
from jax.experimental import pallas as pl
from jax.experimental.pallas import tpu as pltpu
from jax.sharding import Mesh, PartitionSpec as P

TILE = 128
BLK = 24
USED = 8
PANELS = 8
COLS = 16
GROUP = 4
AT = 10
MERGE = PANELS * BLK
END = 2 * MERGE
OWN_ROWS = 32
LIMIT = 12 << 20
PLAN_COST = 32 << 20
TOKEN_COST = 16 << 20
LISTS_COST = 0
SPREAD_COST = 0
DZ = (0, 3, 1, 2)
INNER = [(0, 1), (1, 0), (2, 3), (3, 2)]
OUTER = [(0, 3), (3, 0), (1, 2), (2, 1)]
UP = [(i, (i + 1) % 4) for i in range(4)]
DOWN = [(i, (i + 3) % 4) for i in range(4)]
ACROSS = [(i, (i + 2) % 4) for i in range(4)]
SWAP = [(0, 1), (1, 0)]

SMEM = pl.BlockSpec(memory_space=pltpu.SMEM)
VMEM = pl.BlockSpec(memory_space=pltpu.VMEM)
ANY = pl.BlockSpec(memory_space=pl.ANY)


def split_row(row):
    upper = (row >= BLK).astype(jnp.int32)
    return upper, row - upper * BLK


def used_rows(load):
    mask = jnp.int32(0)
    for t in range(BLK):
        upper, local = split_row(load(t))
        mask = mask | lax.shift_left(jnp.int32(1), local)
    return upper, mask


def spread_kernel(rows, out):
    for i in range(PANELS):
        out[i] = rows[...]


def spread(rows):
    return pl.pallas_call(
        spread_kernel,
        out_shape=jax.ShapeDtypeStruct((PANELS, 1, TILE), jnp.int32),
        in_specs=[VMEM],
        out_specs=VMEM,
        compiler_params=pltpu.CompilerParams(vmem_limit_bytes=1 << 20),
        cost_estimate=pl.CostEstimate(flops=0, bytes_accessed=SPREAD_COST, transcendentals=0),
    )(rows)


def token_kernel(*refs):
    refs[-1][0] = jnp.int32(0)


def token(cost, *arrays):
    return pl.pallas_call(
        token_kernel,
        out_shape=pltpu.SMEM((8,), jnp.int32),
        in_specs=[ANY] * len(arrays),
        out_specs=SMEM,
        compiler_params=pltpu.CompilerParams(vmem_limit_bytes=1 << 20),
        cost_estimate=pl.CostEstimate(flops=cost * 1000, bytes_accessed=cost, transcendentals=0),
    )(*arrays)


def bit(mask, v):
    return lax.shift_right_logical(mask, jnp.int32(v)) & 1


def lists_kernel(pos, req, lists):
    for pair in range(2):
        for dest in range(4):
            base = (pair * 4 + dest) * 16
            upper, mask = used_rows(lambda t: req[dest * 4 + pos[0], pair, t])
            count = jnp.int32(0)
            for v in range(BLK):
                lists[base + count] = jnp.int32(v)
                count = count + bit(mask, v)
            lists[base + 15] = upper
    for n in range(4):
        lists[AT + n] = pos[n]


def make_lists(pos, req):
    return pl.pallas_call(
        lists_kernel,
        out_shape=pltpu.SMEM((128,), jnp.int32),
        in_specs=[SMEM, SMEM],
        out_specs=SMEM,
        compiler_params=pltpu.CompilerParams(vmem_limit_bytes=1 << 20),
        cost_estimate=pl.CostEstimate(flops=0, bytes_accessed=LISTS_COST, transcendentals=0),
    )(pos, req)


def select_own_kernel(lists, _, own, inner, out):
    pair = lists[AT] // 2
    side = lists[AT] % 2
    for dest in range(4):
        base = (pair * 4 + dest) * 16
        upper = lists[base + 15]

        def copy(source):
            for n in range(USED):
                out[dest, n] = source[lists[base + n]]

        pl.when(upper == side)(lambda: copy(own))
        pl.when(upper != side)(lambda: copy(inner))


def select_other_kernel(lists, _, outer, diag, *outs):
    pair = 1 - lists[AT] // 2
    side = (3 - lists[AT]) % 2
    for away in range(4):
        base = (pair * 4 + (lists[AT + 1] + away) % 4) * 16
        upper = lists[base + 15]

        def copy(source, out=outs[away], base=base):
            for n in range(USED):
                out[n] = source[lists[base + n]]

        pl.when(upper == side)(lambda: copy(outer))
        pl.when(upper != side)(lambda: copy(diag))


def select(kernel, out_shape, lists, after, *blocks):
    return pl.pallas_call(
        kernel,
        out_shape=out_shape,
        in_specs=[SMEM, ANY] + [VMEM] * len(blocks),
        out_specs=jax.tree.map(lambda _: VMEM, out_shape),
        compiler_params=pltpu.CompilerParams(vmem_limit_bytes=8 << 20),
        cost_estimate=pl.CostEstimate(flops=0, bytes_accessed=2 << 20, transcendentals=0),
    )(lists, after, *blocks)


def panel_of(pos, at, j):
    z = (pos[at + 2] + DZ[j % 4]) % 4
    pair = pos[at] // 2
    return z, 2 * z + (pair if j < 4 else 1 - pair)


def plan_kernel(pos, rows, req, _, plan, rank):
    uppers = []
    sources = []
    for j in range(PANELS):
        z, panel = panel_of(pos, 0, j)
        upper, mask = used_rows(lambda t: rows[panel, 0, t])
        uppers.append(upper)
        sources.append(z * 4 + 2 * (panel % 2) + upper)
        count = jnp.int32(0)
        for v in range(BLK):
            rank[j * BLK + v] = count
            count = count + bit(mask, v)

    def step(t, carry):
        out_rows = []
        for j in range(PANELS):
            _, panel = panel_of(pos, 0, j)
            local = rows[panel, 0, t] - uppers[j] * BLK
            plan[j * BLK + t] = rank[j * BLK + local]
            out_row = req[sources[j], 0, OWN_ROWS + local]
            place = jnp.int32(j)
            for earlier in reversed(range(j)):
                place = jnp.where(out_rows[earlier] == out_row, earlier, place)
            out_rows.append(out_row)
            plan[MERGE + j * BLK + t] = place
        return carry

    lax.fori_loop(0, BLK, step, 0)
    for n in range(4):
        plan[END + n] = pos[n]


def make_plan(pos, rows, req, after):
    return pl.pallas_call(
        plan_kernel,
        out_shape=pltpu.SMEM((512,), jnp.int32),
        in_specs=[SMEM] * 3 + [ANY],
        out_specs=SMEM,
        scratch_shapes=[pltpu.SMEM((PANELS * BLK,), jnp.int32)],
        compiler_params=pltpu.CompilerParams(vmem_limit_bytes=1 << 20),
        cost_estimate=pl.CostEstimate(flops=0, bytes_accessed=PLAN_COST, transcendentals=0),
    )(pos, rows, req, after)


def products(plan, left, rights, first, n, put):
    for u in range(GROUP):
        t = n * GROUP + u
        for d in range(4):
            j = first + d
            z, _ = panel_of(plan, END, j)
            put(t, j, jnp.dot(left[z, plan[j * BLK + t]], rights[d][t], preferred_element_type=jnp.float32))


def run_both(plan, first, mine, theirs, work):
    same = plan[END] // 2 == plan[END + 3]
    here, there = (mine, theirs) if first == 0 else (theirs, mine)
    pl.when(same)(lambda: work(here))
    pl.when(jnp.logical_not(same))(lambda: work(there))


def own_kernel(plan, left, *refs):
    mine, theirs, (early,) = refs[:4], refs[4:8], refs[8:]

    def work(rights):
        def step(n, carry):
            def put(t, j, product):
                if j == 0:
                    early[t, 0] = product
                else:
                    r = plan[MERGE + j * BLK + t]
                    early[t, r] = jnp.where(r == j, 0.0, early[t, r]) + product

            products(plan, left, rights, 0, n, put)
            return carry

        lax.fori_loop(0, BLK // GROUP, step, 0)

    run_both(plan, 0, mine, theirs, work)


def other_kernel(plan, left0, left1, left2, left3, *refs):
    mine, theirs, (early, merged, totals, left, sums) = refs[:4], refs[4:8], refs[8:]
    for away, piece in enumerate((left0, left1, left2, left3)):
        left[(plan[END + 1] - away) % 4] = piece[...]

    def add_up(n):
        for u in range(GROUP):
            t = n * GROUP + u
            total = jnp.zeros((8, TILE), jnp.float32)
            for j in range(PANELS):
                tile = merged[t, j]
                part = jnp.sum((tile * tile).reshape(16, 8, TILE), axis=0)
                total = total + jnp.where(plan[MERGE + j * BLK + t] == j, part, 0.0)
            sums[pl.ds(t, 1), :] = jnp.sum(total, axis=0, keepdims=True)

    def work(rights):
        def step(n, carry):
            def put(t, j, product):
                r = plan[MERGE + j * BLK + t]
                merged[t, r] = jnp.where(r == j, 0.0, merged[t, r]) + product

            for u in range(GROUP):
                for j in range(4):
                    merged[n * GROUP + u, j] = early[n * GROUP + u, j]
            products(plan, left, rights, 4, n, put)
            add_up(jnp.maximum(n - 1, 0))
            return carry

        lax.fori_loop(0, BLK // GROUP, step, 0)

    run_both(plan, 4, mine, theirs, work)
    add_up(BLK // GROUP - 1)
    for i in range(PANELS):
        totals[i] = sums[...]


EARLY = (BLK, 4, TILE, TILE)
MERGED = (BLK, PANELS, TILE, TILE)


def in_vmem(*arrays):
    return tuple(pltpu.with_memory_space_constraint(a, pltpu.VMEM) for a in arrays)


def multiply_own(plan, left, mine, theirs):
    return pl.pallas_call(
        own_kernel,
        out_shape=pltpu.VMEM(EARLY, jnp.float32),
        in_specs=[SMEM] + [VMEM] * 9,
        out_specs=VMEM,
        compiler_params=pltpu.CompilerParams(vmem_limit_bytes=LIMIT),
        cost_estimate=pl.CostEstimate(flops=2 * 96 * TILE**3, bytes_accessed=16 << 20, transcendentals=0),
    )(plan, *in_vmem(left, *mine, *theirs))


def multiply_other(plan, left, mine, theirs, early):
    return pl.pallas_call(
        other_kernel,
        out_shape=(pltpu.VMEM(MERGED, jnp.float32), pltpu.HBM((PANELS, BLK, TILE), jnp.float32)),
        in_specs=[SMEM] + [VMEM] * 13,
        out_specs=(VMEM, VMEM),
        scratch_shapes=[pltpu.VMEM((4, USED, TILE, TILE), jnp.bfloat16), pltpu.VMEM((BLK, TILE), jnp.float32)],
        compiler_params=pltpu.CompilerParams(vmem_limit_bytes=LIMIT),
        cost_estimate=pl.CostEstimate(flops=2 * 96 * TILE**3, bytes_accessed=16 << 20, transcendentals=0),
    )(plan, *in_vmem(*left, *mine, *theirs, early))


def scale_kernel(plan, merged, totals, out, factor):
    j = pl.program_id(0)

    @pl.when(j == 0)
    def _():
        factor[...] = float(PANELS * PANELS * TILE) / (jnp.sum(totals[...], axis=0) + 1e-6)

    def step(n, carry):
        for u in range(GROUP):
            t = n * GROUP + u
            tile = merged[t, plan[MERGE + j * BLK + t]]
            out[0, t] = (tile * tile * factor[pl.ds(t, 1), :]).astype(jnp.bfloat16)
        return carry

    lax.fori_loop(0, BLK // GROUP, step, 0)


def scale(plan, merged, totals):
    def place(j, plan):
        d = j % 4
        z = (plan[END + 2] + jnp.where(d == 1, 3, jnp.where(d == 2, 1, jnp.where(d == 3, 2, 0)))) % 4
        pair = plan[END] // 2
        return 2 * z + jnp.where(j < 4, pair, 1 - pair), 0, 0, 0

    return pl.pallas_call(
        scale_kernel,
        out_shape=jax.ShapeDtypeStruct((PANELS, BLK, TILE, TILE), jnp.bfloat16),
        grid_spec=pltpu.PrefetchScalarGridSpec(
            num_scalar_prefetch=1,
            grid=(PANELS,),
            in_specs=[VMEM, VMEM],
            out_specs=pl.BlockSpec((1, BLK, TILE, TILE), place),
            scratch_shapes=[pltpu.VMEM((BLK, TILE), jnp.float32)],
        ),
        compiler_params=pltpu.CompilerParams(vmem_limit_bytes=LIMIT),
        cost_estimate=pl.CostEstimate(flops=2 * 192 * TILE**2, bytes_accessed=20 << 20, transcendentals=0),
    )(plan, *in_vmem(merged), totals)


def on_device(tile_values, tile_rows):
    own = tile_values[0]
    pos = jnp.stack([lax.axis_index(a) for a in ("x", "y", "z", "core")]).astype(jnp.int32)
    wide_rows = jnp.pad(tile_rows, ((0, 0), (0, TILE - BLK)))

    inner = lax.ppermute(own, "x", INNER)
    outer = lax.ppermute(own, "x", OUTER)
    rows = lax.all_to_all(spread(wide_rows), ("z", "core"), 0, 0)
    own_rows = jnp.pad(tile_rows, ((0, 0), (OWN_ROWS, TILE - OWN_ROWS - BLK)))
    asks = jnp.broadcast_to(rows.reshape(4, 1, 2, TILE) + own_rows, (4, 4, 2, TILE)).reshape(COLS, 2, TILE)
    req = lax.all_to_all(asks, ("y", "x"), 0, 0)
    own_z, rows_z = lax.optimization_barrier((own, rows))
    below = lax.ppermute(own_z, "z", UP)
    above = lax.ppermute(own_z, "z", DOWN)

    lists = make_lists(pos, req)
    arrived = token(TOKEN_COST, inner, outer)
    send1 = select(select_own_kernel, pltpu.HBM((4, USED, TILE, TILE), jnp.bfloat16), lists, arrived, own, inner)
    left1 = lax.all_to_all(send1, "y", 0, 0)
    diag = lax.ppermute(outer, "x", INNER)

    far = lax.ppermute(below, "z", UP)
    plan = make_plan(pos, rows_z, req, send1)
    sent = pltpu.HBM((USED, TILE, TILE), jnp.bfloat16)
    ready = token(0, left1, plan)
    send2 = select(select_other_kernel, (sent,) * 4, lists, ready, outer, diag)
    kept, far_later = lax.optimization_barrier((send2[0], far))
    left2 = (
        kept,
        lax.ppermute(send2[1], "y", UP),
        lax.ppermute(send2[2], "y", ACROSS),
        lax.ppermute(send2[3], "y", DOWN),
    )

    mine = (own, below, above, far)
    theirs = tuple(lax.ppermute(block, "core", SWAP) for block in (own, below, above, far_later))
    early = multiply_own(plan, left1, mine, theirs)
    merged, totals = multiply_other(plan, left2, mine, theirs, early)
    totals = lax.all_to_all(totals, ("z", "core"), 0, 0)
    return scale(plan, merged, totals)[None]


def solution(mesh):
    fine = Mesh(np.asarray(mesh.devices).reshape(4, 2, 4, 4), ("z", "core", "y", "x"))
    rows, cols = ("z", "core"), ("y", "x")
    return jax.shard_map(
        on_device,
        mesh=fine,
        in_specs=(P(rows, cols, None, None), P(rows, cols)),
        out_specs=P(rows, None, cols, None, None),
        check_vma=False,
    )
```

```python
import jax
import jax.numpy as jnp
import numpy as np
from jax import lax
from jax.experimental import pallas as pl
from jax.experimental.pallas import tpu as pltpu
from jax.sharding import Mesh, PartitionSpec as P

TILE = 128
BLK = 24
USED = 8
PANELS = 8
COLS = 16
GROUP = 4
AT = 10
MERGE = PANELS * BLK
END = 2 * MERGE
OWN_ROWS = 32
LIMIT = 12 << 20
PLAN_COST = 32 << 20
TOKEN_COST = 16
Y1_COST = 0
Y2_COST = 20
DIAG_COST = 20
LISTS_COST = 0
SPREAD_COST = 0
DZ = (0, 3, 1, 2)
INNER = [(0, 1), (1, 0), (2, 3), (3, 2)]
OUTER = [(0, 3), (3, 0), (1, 2), (2, 1)]
UP = [(i, (i + 1) % 4) for i in range(4)]
DOWN = [(i, (i + 3) % 4) for i in range(4)]
ACROSS = [(i, (i + 2) % 4) for i in range(4)]
FAR = [(2 * z, 2 * ((z + 1) % 4)) for z in range(4)] + [(2 * z + 1, 2 * ((z + 3) % 4) + 1) for z in range(4)]
SWAP = [(0, 1), (1, 0)]

SMEM = pl.BlockSpec(memory_space=pltpu.SMEM)
VMEM = pl.BlockSpec(memory_space=pltpu.VMEM)
ANY = pl.BlockSpec(memory_space=pl.ANY)


def split_row(row):
    upper = (row >= BLK).astype(jnp.int32)
    return upper, row - upper * BLK


def used_rows(load):
    mask = jnp.int32(0)
    for t in range(BLK):
        upper, local = split_row(load(t))
        mask = mask | lax.shift_left(jnp.int32(1), local)
    return upper, mask


def spread_kernel(rows, out):
    out[...] = jnp.zeros_like(out)
    for i in range(PANELS):
        out[i, :, :BLK] = rows[...]


def spread(rows):
    return pl.pallas_call(
        spread_kernel,
        out_shape=jax.ShapeDtypeStruct((PANELS, 1, TILE), jnp.int32),
        in_specs=[VMEM],
        out_specs=VMEM,
        compiler_params=pltpu.CompilerParams(vmem_limit_bytes=1 << 20),
        cost_estimate=pl.CostEstimate(flops=0, bytes_accessed=SPREAD_COST, transcendentals=0),
    )(rows)


def token_kernel(*refs):
    refs[-1][0] = jnp.int32(0)


def token(cost, *arrays):
    return pl.pallas_call(
        token_kernel,
        out_shape=pltpu.SMEM((8,), jnp.int32),
        in_specs=[ANY] * len(arrays),
        out_specs=SMEM,
        compiler_params=pltpu.CompilerParams(vmem_limit_bytes=1 << 20),
        cost_estimate=pl.CostEstimate(flops=cost * 10**9, bytes_accessed=0, transcendentals=0),
    )(*arrays)


def bit(mask, v):
    return lax.shift_right_logical(mask, jnp.int32(v)) & 1


def lists_kernel(pos, req, lists):
    for pair in range(2):
        for dest in range(4):
            base = (pair * 4 + dest) * 16
            upper, mask = used_rows(lambda t: req[dest * 4 + pos[0], pair, t])
            count = jnp.int32(0)
            for v in range(BLK):
                lists[base + count] = jnp.int32(v)
                count = count + bit(mask, v)
            lists[base + 15] = upper
    for n in range(4):
        lists[AT + n] = pos[n]


def select_own_kernel(pos, req, own, inner, _, out, lists):
    lists_kernel(pos, req, lists)
    pair = lists[AT] // 2
    side = lists[AT] % 2
    for dest in range(4):
        base = (pair * 4 + dest) * 16
        upper = lists[base + 15]

        def copy(source):
            for n in range(USED):
                out[dest, n] = source[lists[base + n]]

        pl.when(upper == side)(lambda: copy(own))
        pl.when(upper != side)(lambda: copy(inner))


def select_other_kernel(lists, outer, diag, _, __, ___, *outs):
    pair = 1 - lists[AT] // 2
    side = (3 - lists[AT]) % 2
    for away in range(4):
        base = (pair * 4 + (lists[AT + 1] + away) % 4) * 16
        upper = lists[base + 15]

        def copy(source, out=outs[away], base=base):
            for n in range(USED):
                out[n] = source[lists[base + n]]

        pl.when(upper == side)(lambda: copy(outer))
        pl.when(upper != side)(lambda: copy(diag))


def select_own(pos, req, own, inner, after):
    return pl.pallas_call(
        select_own_kernel,
        out_shape=(pltpu.HBM((4, USED, TILE, TILE), jnp.bfloat16), pltpu.SMEM((128,), jnp.int32)),
        in_specs=[SMEM, SMEM, VMEM, VMEM, ANY],
        out_specs=(VMEM, SMEM),
        compiler_params=pltpu.CompilerParams(vmem_limit_bytes=8 << 20),
        cost_estimate=pl.CostEstimate(flops=0, bytes_accessed=2 << 20, transcendentals=0),
    )(pos, req, own, inner, after)


def select(kernel, out_shape, lists, blocks, after):
    return pl.pallas_call(
        kernel,
        out_shape=out_shape,
        in_specs=[SMEM] + [VMEM] * len(blocks) + [ANY] * len(after),
        out_specs=jax.tree.map(lambda _: VMEM, out_shape),
        compiler_params=pltpu.CompilerParams(vmem_limit_bytes=8 << 20),
        cost_estimate=pl.CostEstimate(flops=0, bytes_accessed=2 << 20, transcendentals=0),
    )(lists, *blocks, *after)


def panel_of(pos, at, j):
    z = (pos[at + 2] + DZ[j % 4]) % 4
    pair = pos[at] // 2
    return z, 2 * z + (pair if j < 4 else 1 - pair)


def plan_kernel(pos, rows, req, _, plan, rank):
    uppers = []
    sources = []
    for j in range(PANELS):
        z, panel = panel_of(pos, 0, j)
        upper, mask = used_rows(lambda t: rows[panel, 0, t])
        uppers.append(upper)
        sources.append(z * 4 + 2 * (panel % 2) + upper)
        count = jnp.int32(0)
        for v in range(BLK):
            rank[j * BLK + v] = count
            count = count + bit(mask, v)

    def step(t, carry):
        out_rows = []
        for j in range(PANELS):
            _, panel = panel_of(pos, 0, j)
            local = rows[panel, 0, t] - uppers[j] * BLK
            plan[j * BLK + t] = rank[j * BLK + local]
            out_row = req[sources[j], 0, OWN_ROWS + local]
            place = jnp.int32(j)
            for earlier in reversed(range(j)):
                place = jnp.where(out_rows[earlier] == out_row, earlier, place)
            out_rows.append(out_row)
            plan[MERGE + j * BLK + t] = place
        return carry

    lax.fori_loop(0, BLK, step, 0)
    for n in range(4):
        plan[END + n] = pos[n]


def make_plan(pos, rows, req, after):
    return pl.pallas_call(
        plan_kernel,
        out_shape=pltpu.SMEM((512,), jnp.int32),
        in_specs=[SMEM] * 3 + [ANY],
        out_specs=SMEM,
        scratch_shapes=[pltpu.SMEM((PANELS * BLK,), jnp.int32)],
        compiler_params=pltpu.CompilerParams(vmem_limit_bytes=1 << 20),
        cost_estimate=pl.CostEstimate(flops=0, bytes_accessed=PLAN_COST, transcendentals=0),
    )(pos, rows, req, after)


def products(plan, left, rights, places, n, put):
    for u in range(GROUP):
        t = n * GROUP + u
        for j in places:
            z, _ = panel_of(plan, END, j)
            product = jnp.dot(left[z, plan[j * BLK + t]], rights[j % 4][t], preferred_element_type=jnp.float32)
            put(t, j, product)


def run_both(plan, mine, theirs, work):
    same = plan[END] // 2 == plan[END + 3]
    pl.when(same)(lambda: work(mine, theirs))
    pl.when(jnp.logical_not(same))(lambda: work(theirs, mine))


def own_kernel(plan, left, *refs):
    mine, theirs, early = refs[:3], refs[3:6], refs[7]

    def work(rights, _):
        def step(n, carry):
            def put(t, j, product):
                if j == 0:
                    early[t, 0] = product
                else:
                    r = plan[MERGE + j * BLK + t]
                    early[t, r] = jnp.where(r == j, 0.0, early[t, r]) + product

            products(plan, left, rights, range(3), n, put)
            return carry

        lax.fori_loop(0, BLK // GROUP, step, 0)

    run_both(plan, mine, theirs, work)


def other_kernel(plan, own_left, left0, left1, left2, left3, *refs):
    mine, theirs, (early, _, merged, totals, left, sums) = refs[:4], refs[4:8], refs[8:]
    for away, piece in enumerate((left0, left1, left2, left3)):
        left[(plan[END + 1] - away) % 4] = piece[...]

    def add_up(n):
        for u in range(GROUP):
            t = n * GROUP + u
            total = jnp.zeros((8, TILE), jnp.float32)
            for j in range(PANELS):
                tile = merged[t, j]
                part = jnp.sum((tile * tile).reshape(16, 8, TILE), axis=0)
                total = total + jnp.where(plan[MERGE + j * BLK + t] == j, part, 0.0)
            sums[pl.ds(t, 1), :] = jnp.sum(total, axis=0, keepdims=True)

    def work(own_rights, rights):
        def step(n, carry):
            def put(t, j, product):
                r = plan[MERGE + j * BLK + t]
                merged[t, r] = jnp.where(r == j, 0.0, merged[t, r]) + product

            for u in range(GROUP):
                for j in range(3):
                    merged[n * GROUP + u, j] = early[n * GROUP + u, j]
            products(plan, own_left, own_rights, (3,), n, put)
            products(plan, left, rights, range(4, PANELS), n, put)
            add_up(jnp.maximum(n - 1, 0))
            return carry

        lax.fori_loop(0, BLK // GROUP, step, 0)

    run_both(plan, mine, theirs, work)
    add_up(BLK // GROUP - 1)
    for i in range(PANELS):
        totals[i] = sums[...]


EARLY = (BLK, 3, TILE, TILE)
MERGED = (BLK, PANELS, TILE, TILE)


def in_vmem(*arrays):
    return tuple(pltpu.with_memory_space_constraint(a, pltpu.VMEM) for a in arrays)


def multiply_own(plan, left, mine, theirs, after):
    return pl.pallas_call(
        own_kernel,
        out_shape=pltpu.VMEM(EARLY, jnp.float32),
        in_specs=[SMEM] + [VMEM] * 7 + [ANY],
        out_specs=VMEM,
        compiler_params=pltpu.CompilerParams(vmem_limit_bytes=LIMIT),
        cost_estimate=pl.CostEstimate(flops=2 * 96 * TILE**3, bytes_accessed=16 << 20, transcendentals=0),
    )(plan, *in_vmem(left, *mine, *theirs), after)


def multiply_other(plan, own_left, left, mine, theirs, early):
    return pl.pallas_call(
        other_kernel,
        out_shape=(pltpu.VMEM(MERGED, jnp.float32), pltpu.HBM((PANELS, BLK, TILE), jnp.float32)),
        in_specs=[SMEM] + [VMEM] * 14 + [ANY],
        out_specs=(VMEM, VMEM),
        scratch_shapes=[pltpu.VMEM((4, USED, TILE, TILE), jnp.bfloat16), pltpu.VMEM((BLK, TILE), jnp.float32)],
        compiler_params=pltpu.CompilerParams(vmem_limit_bytes=LIMIT),
        cost_estimate=pl.CostEstimate(flops=2 * 96 * TILE**3, bytes_accessed=16 << 20, transcendentals=0),
    )(plan, *in_vmem(own_left, *left, *mine, *theirs, early), token(Y2_COST, *left[1:]))


def scale_kernel(plan, merged, totals, out, factor):
    d = pl.program_id(0)
    pair = plan[END] // 2

    @pl.when(d == 0)
    def _():
        factor[...] = float(PANELS * PANELS * TILE) / (jnp.sum(totals[...], axis=0) + 1e-6)

    def step(n, carry):
        for u in range(GROUP):
            t = n * GROUP + u
            scaling = factor[pl.ds(t, 1), :]
            for half in range(2):
                tile = merged[t, plan[MERGE + (half * 4 + d) * BLK + t]]
                out[pair if half == 0 else 1 - pair, t] = (tile * tile * scaling).astype(jnp.bfloat16)
        return carry

    lax.fori_loop(0, BLK // GROUP, step, 0)


def scale(plan, merged, totals):
    def place(d, plan):
        away = jnp.where(d == 1, 3, jnp.where(d == 2, 1, jnp.where(d == 3, 2, 0)))
        return (plan[END + 2] + away) % 4, 0, 0, 0

    return pl.pallas_call(
        scale_kernel,
        out_shape=jax.ShapeDtypeStruct((PANELS, BLK, TILE, TILE), jnp.bfloat16),
        grid_spec=pltpu.PrefetchScalarGridSpec(
            num_scalar_prefetch=1,
            grid=(4,),
            in_specs=[VMEM, VMEM],
            out_specs=pl.BlockSpec((2, BLK, TILE, TILE), place),
            scratch_shapes=[pltpu.VMEM((BLK, TILE), jnp.float32)],
        ),
        compiler_params=pltpu.CompilerParams(vmem_limit_bytes=LIMIT),
        cost_estimate=pl.CostEstimate(flops=2 * 192 * TILE**2, bytes_accessed=20 << 20, transcendentals=0),
    )(plan, *in_vmem(merged), totals)


def on_device(tile_values, tile_rows):
    own = tile_values[0]
    pos = jnp.stack([lax.axis_index(a) for a in ("x", "y", "z", "core")]).astype(jnp.int32)
    inner = lax.ppermute(own, "x", INNER)
    outer = lax.ppermute(own, "x", OUTER)
    rows = lax.all_to_all(spread(tile_rows), ("z", "core"), 0, 0)
    own_rows = jnp.pad(tile_rows, ((0, 0), (OWN_ROWS, TILE - OWN_ROWS - BLK)))
    asks = jnp.broadcast_to(rows.reshape(4, 1, 2, TILE) + own_rows, (4, 4, 2, TILE)).reshape(COLS, 2, TILE)
    req = lax.all_to_all(asks, ("y", "x"), 0, 0)
    own_z, rows_z = lax.optimization_barrier((own, rows))
    below = lax.ppermute(own_z, "z", UP)
    above = lax.ppermute(own_z, "z", DOWN)

    arrived = token(TOKEN_COST, inner, outer)
    send1, lists = select_own(pos, req, own, inner, arrived)
    left1 = lax.all_to_all(send1, "y", 0, 0)
    diag = lax.ppermute(outer, "x", INNER)

    far = lax.ppermute(jnp.where(lax.axis_index("core") == 0, below, above), ("z", "core"), FAR)
    plan = make_plan(pos, rows_z, req, send1)
    sent = pltpu.HBM((USED, TILE, TILE), jnp.bfloat16)
    after = (token(Y1_COST, left1), token(DIAG_COST, diag), plan)
    send2 = select(select_other_kernel, (sent,) * 4, lists, (outer, diag), after)
    left2 = (
        send2[0],
        lax.ppermute(send2[1], "y", UP),
        lax.ppermute(send2[2], "y", ACROSS),
        lax.ppermute(send2[3], "y", DOWN),
    )

    mine = (own, below, above)
    theirs = tuple(lax.ppermute(block, "core", SWAP) for block in mine)
    early = multiply_own(plan, left1, mine, theirs, send2[0])
    early, far = lax.optimization_barrier((early, far))
    mine, theirs = (*mine, far), (*theirs, lax.ppermute(far, "core", SWAP))
    merged, totals = multiply_other(plan, left1, left2, mine, theirs, early)
    totals = lax.all_to_all(totals, ("z", "core"), 0, 0)
    return scale(plan, merged, totals)[None]


def solution(mesh):
    fine = Mesh(np.asarray(mesh.devices).reshape(4, 2, 4, 4), ("z", "core", "y", "x"))
    rows, cols = ("z", "core"), ("y", "x")
    return jax.shard_map(
        on_device,
        mesh=fine,
        in_specs=(P(rows, cols, None, None), P(rows, cols)),
        out_specs=P(rows, None, cols, None, None),
        check_vma=False,
    )
```

```python
import jax
import jax.numpy as jnp
import numpy as np
from jax import lax
from jax.experimental import pallas as pl
from jax.experimental.pallas import tpu as pltpu
from jax.sharding import Mesh, PartitionSpec as P

TILE = 128
BLK = 24
USED = 8
PANELS = 8
COLS = 16
GROUP = 4
AT = 10
MERGE = PANELS * BLK
END = 2 * MERGE
OWN_ROWS = 32
LIMIT = 12 << 20
PLAN_COST = 32 << 20
TOKEN_COST = 16
Y1_COST = 0
Y1_LATE_COST = 60
Y2_COST = 20
DIAG_COST = 20
LISTS_COST = 0
DZ = (0, 3, 1, 2)
INNER = [(0, 1), (1, 0), (2, 3), (3, 2)]
OUTER = [(0, 3), (3, 0), (1, 2), (2, 1)]
UP = [(i, (i + 1) % 4) for i in range(4)]
DOWN = [(i, (i + 3) % 4) for i in range(4)]
ACROSS = [(i, (i + 2) % 4) for i in range(4)]
FAR = [(2 * z, 2 * ((z + 1) % 4)) for z in range(4)] + [(2 * z + 1, 2 * ((z + 3) % 4) + 1) for z in range(4)]
SWAP = [(0, 1), (1, 0)]

SMEM = pl.BlockSpec(memory_space=pltpu.SMEM)
VMEM = pl.BlockSpec(memory_space=pltpu.VMEM)
ANY = pl.BlockSpec(memory_space=pl.ANY)


def split_row(row):
    upper = (row >= BLK).astype(jnp.int32)
    return upper, row - upper * BLK


def used_rows(load):
    mask = jnp.int32(0)
    for t in range(BLK):
        upper, local = split_row(load(t))
        mask = mask | lax.shift_left(jnp.int32(1), local)
    return upper, mask


def token_kernel(*refs):
    refs[-1][0] = jnp.int32(0)


def token(cost, *arrays):
    return pl.pallas_call(
        token_kernel,
        out_shape=pltpu.SMEM((8,), jnp.int32),
        in_specs=[ANY] * len(arrays),
        out_specs=SMEM,
        compiler_params=pltpu.CompilerParams(vmem_limit_bytes=1 << 20),
        cost_estimate=pl.CostEstimate(flops=cost * 10**9, bytes_accessed=0, transcendentals=0),
    )(*arrays)


def bit(mask, v):
    return lax.shift_right_logical(mask, jnp.int32(v)) & 1


def lists_kernel(pos, req, lists):
    for pair in range(2):
        for dest in range(4):
            base = (pair * 4 + dest) * 16
            upper, mask = used_rows(lambda t: req[dest * 4 + pos[0], pair, t])
            count = jnp.int32(0)
            for v in range(BLK):
                lists[base + count] = jnp.int32(v)
                count = count + bit(mask, v)
            lists[base + 15] = upper
    for n in range(4):
        lists[AT + n] = pos[n]


def select_own_kernel(pos, req, own, inner, _, *refs):
    outs, lists = refs[:4], refs[4]
    lists_kernel(pos, req, lists)
    pair = lists[AT] // 2
    side = lists[AT] % 2
    for away in range(4):
        base = (pair * 4 + (lists[AT + 1] + away) % 4) * 16
        upper = lists[base + 15]

        def copy(source, out=outs[away], base=base):
            for n in range(USED):
                out[n] = source[lists[base + n]]

        pl.when(upper == side)(lambda: copy(own))
        pl.when(upper != side)(lambda: copy(inner))


def select_other_kernel(lists, outer, diag, _, __, ___, *outs):
    pair = 1 - lists[AT] // 2
    side = (3 - lists[AT]) % 2
    for away in range(4):
        base = (pair * 4 + (lists[AT + 1] + away) % 4) * 16
        upper = lists[base + 15]

        def copy(source, out=outs[away], base=base):
            for n in range(USED):
                out[n] = source[lists[base + n]]

        pl.when(upper == side)(lambda: copy(outer))
        pl.when(upper != side)(lambda: copy(diag))


def select_own(pos, req, own, inner, after):
    return pl.pallas_call(
        select_own_kernel,
        out_shape=(pltpu.HBM((USED, TILE, TILE), jnp.bfloat16),) * 4 + (pltpu.SMEM((128,), jnp.int32),),
        in_specs=[SMEM, SMEM, VMEM, VMEM, ANY],
        out_specs=(VMEM,) * 4 + (SMEM,),
        compiler_params=pltpu.CompilerParams(vmem_limit_bytes=8 << 20),
        cost_estimate=pl.CostEstimate(flops=0, bytes_accessed=2 << 20, transcendentals=0),
    )(pos, req, own, inner, after)


def select(kernel, out_shape, lists, blocks, after):
    return pl.pallas_call(
        kernel,
        out_shape=out_shape,
        in_specs=[SMEM] + [VMEM] * len(blocks) + [ANY] * len(after),
        out_specs=jax.tree.map(lambda _: VMEM, out_shape),
        compiler_params=pltpu.CompilerParams(vmem_limit_bytes=8 << 20),
        cost_estimate=pl.CostEstimate(flops=0, bytes_accessed=2 << 20, transcendentals=0),
    )(lists, *blocks, *after)


def panel_of(pos, at, j):
    z = (pos[at + 2] + DZ[j % 4]) % 4
    pair = pos[at] // 2
    return z, 2 * z + (pair if j < 4 else 1 - pair)


def plan_kernel(pos, rows, req, _, plan, rank):
    uppers = []
    sources = []
    for j in range(PANELS):
        z, panel = panel_of(pos, 0, j)
        upper, mask = used_rows(lambda t: rows[panel, 0, t])
        uppers.append(upper)
        sources.append(z * 4 + 2 * (panel % 2) + upper)
        count = jnp.int32(0)
        for v in range(BLK):
            rank[j * BLK + v] = count
            count = count + bit(mask, v)

    def step(t, carry):
        out_rows = []
        for j in range(PANELS):
            _, panel = panel_of(pos, 0, j)
            local = rows[panel, 0, t] - uppers[j] * BLK
            plan[j * BLK + t] = rank[j * BLK + local]
            out_row = req[sources[j], 0, OWN_ROWS + local]
            place = jnp.int32(j)
            for earlier in reversed(range(j)):
                place = jnp.where(out_rows[earlier] == out_row, earlier, place)
            out_rows.append(out_row)
            plan[MERGE + j * BLK + t] = place
        return carry

    lax.fori_loop(0, BLK, step, 0)
    for n in range(4):
        plan[END + n] = pos[n]


def make_plan(pos, rows, req, after):
    return pl.pallas_call(
        plan_kernel,
        out_shape=pltpu.SMEM((512,), jnp.int32),
        in_specs=[SMEM] * 3 + [ANY],
        out_specs=SMEM,
        scratch_shapes=[pltpu.SMEM((PANELS * BLK,), jnp.int32)],
        compiler_params=pltpu.CompilerParams(vmem_limit_bytes=1 << 20),
        cost_estimate=pl.CostEstimate(flops=0, bytes_accessed=PLAN_COST, transcendentals=0),
    )(pos, rows, req, after)


def products(plan, left, rights, places, n, put):
    for u in range(GROUP):
        t = n * GROUP + u
        for j in places:
            z, _ = panel_of(plan, END, j)
            product = jnp.dot(left[z, plan[j * BLK + t]], rights[j % 4][t], preferred_element_type=jnp.float32)
            put(t, j, product)


def run_both(plan, mine, theirs, work):
    same = plan[END] // 2 == plan[END + 3]
    pl.when(same)(lambda: work(mine, theirs))
    pl.when(jnp.logical_not(same))(lambda: work(theirs, mine))


def gather(plan, pieces, left):
    for away, piece in enumerate(pieces):
        left[(plan[END + 1] - away) % 4] = piece[...]


def own_kernel(plan, *refs):
    pieces, mine, theirs, (_, _, early, left) = refs[:4], refs[4:7], refs[7:10], refs[10:]
    gather(plan, pieces, left)

    def work(rights, _):
        def step(n, carry):
            def put(t, j, product):
                if j == 0:
                    early[t, 0] = product
                else:
                    r = plan[MERGE + j * BLK + t]
                    early[t, r] = jnp.where(r == j, 0.0, early[t, r]) + product

            products(plan, left, rights, range(3), n, put)
            return carry

        lax.fori_loop(0, BLK // GROUP, step, 0)

    run_both(plan, mine, theirs, work)


def other_kernel(plan, *refs):
    own_pieces, pieces, mine, theirs = refs[:4], refs[4:8], refs[8:12], refs[12:16]
    early, _, merged, totals, own_left, left, sums = refs[16:]
    gather(plan, own_pieces, own_left)
    gather(plan, pieces, left)

    def add_up(n):
        for u in range(GROUP):
            t = n * GROUP + u
            total = jnp.zeros((8, TILE), jnp.float32)
            for j in range(PANELS):
                tile = merged[t, j]
                part = jnp.sum((tile * tile).reshape(16, 8, TILE), axis=0)
                total = total + jnp.where(plan[MERGE + j * BLK + t] == j, part, 0.0)
            sums[pl.ds(t, 1), :] = jnp.sum(total, axis=0, keepdims=True)

    def work(own_rights, rights):
        def step(n, carry):
            def put(t, j, product):
                r = plan[MERGE + j * BLK + t]
                merged[t, r] = jnp.where(r == j, 0.0, merged[t, r]) + product

            for u in range(GROUP):
                for j in range(3):
                    merged[n * GROUP + u, j] = early[n * GROUP + u, j]
            products(plan, own_left, own_rights, (3,), n, put)
            products(plan, left, rights, range(4, PANELS), n, put)
            add_up(jnp.maximum(n - 1, 0))
            return carry

        lax.fori_loop(0, BLK // GROUP, step, 0)

    run_both(plan, mine, theirs, work)
    add_up(BLK // GROUP - 1)
    for i in range(PANELS):
        totals[i] = sums[...]


EARLY = (BLK, 3, TILE, TILE)
MERGED = (BLK, PANELS, TILE, TILE)
LEFT = pltpu.VMEM((4, USED, TILE, TILE), jnp.bfloat16)


def in_vmem(*arrays):
    return tuple(pltpu.with_memory_space_constraint(a, pltpu.VMEM) for a in arrays)


def multiply_own(plan, left, mine, theirs, after):
    return pl.pallas_call(
        own_kernel,
        out_shape=pltpu.VMEM(EARLY, jnp.float32),
        in_specs=[SMEM] + [VMEM] * 10 + [ANY] * 2,
        out_specs=VMEM,
        scratch_shapes=[LEFT],
        compiler_params=pltpu.CompilerParams(vmem_limit_bytes=LIMIT),
        cost_estimate=pl.CostEstimate(flops=2 * 96 * TILE**3, bytes_accessed=16 << 20, transcendentals=0),
    )(plan, *in_vmem(*left, *mine, *theirs), *after)


def multiply_other(plan, own_left, left, mine, theirs, early):
    return pl.pallas_call(
        other_kernel,
        out_shape=(pltpu.VMEM(MERGED, jnp.float32), pltpu.HBM((PANELS, BLK, TILE), jnp.float32)),
        in_specs=[SMEM] + [VMEM] * 17 + [ANY],
        out_specs=(VMEM, VMEM),
        scratch_shapes=[LEFT, LEFT, pltpu.VMEM((BLK, TILE), jnp.float32)],
        compiler_params=pltpu.CompilerParams(vmem_limit_bytes=LIMIT),
        cost_estimate=pl.CostEstimate(flops=2 * 96 * TILE**3, bytes_accessed=16 << 20, transcendentals=0),
    )(plan, *in_vmem(*own_left, *left, *mine, *theirs, early), token(Y2_COST, *left[1:]))


def scale_kernel(plan, merged, totals, out, factor):
    d = pl.program_id(0)
    pair = plan[END] // 2

    @pl.when(d == 0)
    def _():
        factor[...] = float(PANELS * PANELS * TILE) / (jnp.sum(totals[...], axis=0) + 1e-6)

    def step(n, carry):
        for u in range(GROUP):
            t = n * GROUP + u
            scaling = factor[pl.ds(t, 1), :]
            for half in range(2):
                tile = merged[t, plan[MERGE + (half * 4 + d) * BLK + t]]
                out[pair if half == 0 else 1 - pair, t] = (tile * tile * scaling).astype(jnp.bfloat16)
        return carry

    lax.fori_loop(0, BLK // GROUP, step, 0)


def scale(plan, merged, totals):
    def place(d, plan):
        away = jnp.where(d == 1, 3, jnp.where(d == 2, 1, jnp.where(d == 3, 2, 0)))
        return (plan[END + 2] + away) % 4, 0, 0, 0

    return pl.pallas_call(
        scale_kernel,
        out_shape=jax.ShapeDtypeStruct((PANELS, BLK, TILE, TILE), jnp.bfloat16),
        grid_spec=pltpu.PrefetchScalarGridSpec(
            num_scalar_prefetch=1,
            grid=(4,),
            in_specs=[VMEM, VMEM],
            out_specs=pl.BlockSpec((2, BLK, TILE, TILE), place),
            scratch_shapes=[pltpu.VMEM((BLK, TILE), jnp.float32)],
        ),
        compiler_params=pltpu.CompilerParams(vmem_limit_bytes=LIMIT),
        cost_estimate=pl.CostEstimate(flops=2 * 192 * TILE**2, bytes_accessed=20 << 20, transcendentals=0),
    )(plan, *in_vmem(merged), totals)


def exchange(send):
    return (send[0],) + tuple(lax.ppermute(part, "y", way) for part, way in zip(send[1:], (UP, ACROSS, DOWN)))


def on_device(tile_values, tile_rows):
    own = tile_values[0]
    pos = jnp.stack([lax.axis_index(a) for a in ("x", "y", "z", "core")]).astype(jnp.int32)
    inner = lax.ppermute(own, "x", INNER)
    outer = lax.ppermute(own, "x", OUTER)
    wide_rows = jnp.pad(tile_rows, ((0, 0), (0, TILE - BLK)))
    rows = lax.all_to_all(jnp.broadcast_to(wide_rows, (PANELS, 1, TILE)), ("z", "core"), 0, 0)
    own_rows = jnp.pad(tile_rows, ((0, 0), (OWN_ROWS, TILE - OWN_ROWS - BLK)))
    asks = jnp.broadcast_to(rows.reshape(4, 1, 2, TILE) + own_rows, (4, 4, 2, TILE)).reshape(COLS, 2, TILE)
    req = lax.all_to_all(asks, ("y", "x"), 0, 0)
    own_z, rows_z = lax.optimization_barrier((own, rows))
    below = lax.ppermute(own_z, "z", UP)
    above = lax.ppermute(own_z, "z", DOWN)

    arrived = token(TOKEN_COST, inner, outer)
    *send1, lists = select_own(pos, req, own, inner, arrived)
    left1 = exchange(send1)
    diag = lax.ppermute(outer, "x", INNER)

    far = lax.ppermute(jnp.where(lax.axis_index("core") == 0, below, above), ("z", "core"), FAR)
    plan = make_plan(pos, rows_z, req, diag)
    sent = pltpu.HBM((USED, TILE, TILE), jnp.bfloat16)
    after = (token(Y1_COST, left1[1]), token(DIAG_COST, diag), lists)
    send2 = select(select_other_kernel, (sent,) * 4, lists, (outer, diag), after)
    left2 = exchange(send2)
    mine = (own, below, above)
    kept, *later = lax.optimization_barrier((send2[0], *mine))
    theirs = tuple(lax.ppermute(block, "core", SWAP) for block in later)
    left2 = (kept, *left2[1:])
    early = multiply_own(plan, left1, mine, theirs, (kept, token(Y1_LATE_COST, *left1[2:])))
    kept2, far = lax.optimization_barrier((kept, far))
    left2 = (kept2, *left2[1:])
    mine, theirs = (*mine, far), (*theirs, lax.ppermute(far, "core", SWAP))
    merged, totals = multiply_other(plan, left1, left2, mine, theirs, early)
    totals = lax.all_to_all(totals, ("z", "core"), 0, 0)
    return scale(plan, merged, totals)[None]


def solution(mesh):
    fine = Mesh(np.asarray(mesh.devices).reshape(4, 2, 4, 4), ("z", "core", "y", "x"))
    rows, cols = ("z", "core"), ("y", "x")
    return jax.shard_map(
        on_device,
        mesh=fine,
        in_specs=(P(rows, cols, None, None), P(rows, cols)),
        out_specs=P(rows, None, cols, None, None),
        check_vma=False,
    )
```

```python
import jax
import jax.numpy as jnp
import numpy as np
from jax import lax
from jax.experimental import pallas as pl
from jax.experimental.pallas import tpu as pltpu
from jax.sharding import Mesh, PartitionSpec as P

TILE = 128
BLK = 24
USED = 8
PANELS = 8
COLS = 16
GROUP = 4
AT = 10
MERGE = PANELS * BLK
END = 2 * MERGE
OWN_ROWS = 32
LIMIT = 12 << 20
PLAN_COST = 32 << 20
TOKEN_COST = 16
Y1_COST = 0
Y1_LATE_COST = 60
Y2_COST = 20
DIAG_COST = 20
LISTS_COST = 0
DZ = (0, 3, 1, 2)
INNER = [(0, 1), (1, 0), (2, 3), (3, 2)]
OUTER = [(0, 3), (3, 0), (1, 2), (2, 1)]
UP = [(i, (i + 1) % 4) for i in range(4)]
DOWN = [(i, (i + 3) % 4) for i in range(4)]
ACROSS = [(i, (i + 2) % 4) for i in range(4)]
FAR = [(2 * z, 2 * ((z + 1) % 4)) for z in range(4)] + [(2 * z + 1, 2 * ((z + 3) % 4) + 1) for z in range(4)]
SWAP = [(0, 1), (1, 0)]

SMEM = pl.BlockSpec(memory_space=pltpu.SMEM)
VMEM = pl.BlockSpec(memory_space=pltpu.VMEM)
ANY = pl.BlockSpec(memory_space=pl.ANY)


def split_row(row):
    upper = (row >= BLK).astype(jnp.int32)
    return upper, row - upper * BLK


def used_rows(load):
    mask = jnp.int32(0)
    for t in range(BLK):
        upper, local = split_row(load(t))
        mask = mask | lax.shift_left(jnp.int32(1), local)
    return upper, mask


def token_kernel(*refs):
    refs[-1][0] = jnp.int32(0)


def token(cost, *arrays):
    return pl.pallas_call(
        token_kernel,
        out_shape=pltpu.SMEM((8,), jnp.int32),
        in_specs=[ANY] * len(arrays),
        out_specs=SMEM,
        compiler_params=pltpu.CompilerParams(vmem_limit_bytes=1 << 20),
        cost_estimate=pl.CostEstimate(flops=cost * 10**9, bytes_accessed=0, transcendentals=0),
    )(*arrays)


def bit(mask, v):
    return lax.shift_right_logical(mask, jnp.int32(v)) & 1


def lists_kernel(pos, req, lists):
    for pair in range(2):
        for dest in range(4):
            base = (pair * 4 + dest) * 16
            upper, mask = used_rows(lambda t: req[dest * 4 + pos[0], pair, t])
            count = jnp.int32(0)
            for v in range(BLK):
                lists[base + count] = jnp.int32(v)
                count = count + bit(mask, v)
            lists[base + 15] = upper
    for n in range(4):
        lists[AT + n] = pos[n]


def select_own_kernel(pos, req, own, inner, _, *refs):
    outs, lists = refs[:4], refs[4]
    lists_kernel(pos, req, lists)
    pair = lists[AT] // 2
    side = lists[AT] % 2
    for away in range(4):
        base = (pair * 4 + (lists[AT + 1] + away) % 4) * 16
        upper = lists[base + 15]

        def copy(source, out=outs[away], base=base):
            for n in range(USED):
                out[n] = source[lists[base + n]]

        pl.when(upper == side)(lambda: copy(own))
        pl.when(upper != side)(lambda: copy(inner))


def select_other_kernel(lists, outer, diag, _, __, ___, *outs):
    pair = 1 - lists[AT] // 2
    side = (3 - lists[AT]) % 2
    for away in range(4):
        base = (pair * 4 + (lists[AT + 1] + away) % 4) * 16
        upper = lists[base + 15]

        def copy(source, out=outs[away], base=base):
            for n in range(USED):
                out[n] = source[lists[base + n]]

        pl.when(upper == side)(lambda: copy(outer))
        pl.when(upper != side)(lambda: copy(diag))


def select_own(pos, req, own, inner, after):
    return pl.pallas_call(
        select_own_kernel,
        out_shape=(pltpu.HBM((USED, TILE, TILE), jnp.bfloat16),) * 4 + (pltpu.SMEM((128,), jnp.int32),),
        in_specs=[SMEM, SMEM, VMEM, VMEM, ANY],
        out_specs=(VMEM,) * 4 + (SMEM,),
        compiler_params=pltpu.CompilerParams(vmem_limit_bytes=8 << 20),
        cost_estimate=pl.CostEstimate(flops=0, bytes_accessed=2 << 20, transcendentals=0),
    )(pos, req, own, inner, after)


def select(kernel, out_shape, lists, blocks, after):
    return pl.pallas_call(
        kernel,
        out_shape=out_shape,
        in_specs=[SMEM] + [VMEM] * len(blocks) + [ANY] * len(after),
        out_specs=jax.tree.map(lambda _: VMEM, out_shape),
        compiler_params=pltpu.CompilerParams(vmem_limit_bytes=8 << 20),
        cost_estimate=pl.CostEstimate(flops=0, bytes_accessed=2 << 20, transcendentals=0),
    )(lists, *blocks, *after)


def panel_of(pos, at, j):
    z = (pos[at + 2] + DZ[j % 4]) % 4
    pair = pos[at] // 2
    return z, 2 * z + (pair if j < 4 else 1 - pair)


def plan_kernel(pos, rows, req, _, plan, rank):
    uppers = []
    sources = []
    for j in range(PANELS):
        z, panel = panel_of(pos, 0, j)
        upper, mask = used_rows(lambda t: rows[panel, 0, t])
        uppers.append(upper)
        sources.append(z * 4 + 2 * (panel % 2) + upper)
        count = jnp.int32(0)
        for v in range(BLK):
            rank[j * BLK + v] = count
            count = count + bit(mask, v)

    def step(t, carry):
        out_rows = []
        for j in range(PANELS):
            _, panel = panel_of(pos, 0, j)
            local = rows[panel, 0, t] - uppers[j] * BLK
            plan[j * BLK + t] = rank[j * BLK + local]
            out_row = req[sources[j], 0, OWN_ROWS + local]
            place = jnp.int32(j)
            for earlier in reversed(range(j)):
                place = jnp.where(out_rows[earlier] == out_row, earlier, place)
            out_rows.append(out_row)
            plan[MERGE + j * BLK + t] = place
        return carry

    lax.fori_loop(0, BLK, step, 0)
    for n in range(4):
        plan[END + n] = pos[n]


def make_plan(pos, rows, req, after):
    return pl.pallas_call(
        plan_kernel,
        out_shape=pltpu.SMEM((512,), jnp.int32),
        in_specs=[SMEM] * 3 + [ANY],
        out_specs=SMEM,
        scratch_shapes=[pltpu.SMEM((PANELS * BLK,), jnp.int32)],
        compiler_params=pltpu.CompilerParams(vmem_limit_bytes=1 << 20),
        cost_estimate=pl.CostEstimate(flops=0, bytes_accessed=PLAN_COST, transcendentals=0),
    )(pos, rows, req, after)


def products(plan, left, rights, places, n, put):
    for u in range(GROUP):
        t = n * GROUP + u
        for j in places:
            z, _ = panel_of(plan, END, j)
            product = jnp.dot(left[z, plan[j * BLK + t]], rights[j % 4][t], preferred_element_type=jnp.float32)
            put(t, j, product)


def run_both(plan, mine, theirs, work):
    same = plan[END] // 2 == plan[END + 3]
    pl.when(same)(lambda: work(mine, theirs))
    pl.when(jnp.logical_not(same))(lambda: work(theirs, mine))


def gather(plan, pieces, left):
    for away, piece in enumerate(pieces):
        left[(plan[END + 1] - away) % 4] = piece[...]


def own_kernel(plan, *refs):
    pieces, mine, theirs, (_, _, early, done, left) = refs[:4], refs[4:7], refs[7:10], refs[10:]
    done[0] = jnp.int32(0)
    gather(plan, pieces, left)

    def work(rights, _):
        def step(n, carry):
            def put(t, j, product):
                if j == 0:
                    early[t, 0] = product
                else:
                    r = plan[MERGE + j * BLK + t]
                    early[t, r] = jnp.where(r == j, 0.0, early[t, r]) + product

            products(plan, left, rights, range(3), n, put)
            return carry

        lax.fori_loop(0, BLK // GROUP, step, 0)

    run_both(plan, mine, theirs, work)


def other_kernel(plan, *refs):
    own_pieces, pieces, mine, theirs = refs[:4], refs[4:8], refs[8:12], refs[12:16]
    early, _, merged, totals, own_left, left, sums = refs[16:]
    gather(plan, own_pieces, own_left)
    gather(plan, pieces, left)

    def add_up(n):
        for u in range(GROUP):
            t = n * GROUP + u
            total = jnp.zeros((8, TILE), jnp.float32)
            for j in range(PANELS):
                tile = merged[t, j]
                part = jnp.sum((tile * tile).reshape(16, 8, TILE), axis=0)
                total = total + jnp.where(plan[MERGE + j * BLK + t] == j, part, 0.0)
            sums[pl.ds(t, 1), :] = jnp.sum(total, axis=0, keepdims=True)

    def work(own_rights, rights):
        def step(n, carry):
            def put(t, j, product):
                r = plan[MERGE + j * BLK + t]
                merged[t, r] = jnp.where(r == j, 0.0, merged[t, r]) + product

            for u in range(GROUP):
                for j in range(3):
                    merged[n * GROUP + u, j] = early[n * GROUP + u, j]
            products(plan, own_left, own_rights, (3,), n, put)
            products(plan, left, rights, range(4, PANELS), n, put)
            add_up(jnp.maximum(n - 1, 0))
            return carry

        lax.fori_loop(0, BLK // GROUP, step, 0)

    run_both(plan, mine, theirs, work)
    add_up(BLK // GROUP - 1)
    for i in range(PANELS):
        totals[i] = sums[...]


EARLY = (BLK, 3, TILE, TILE)
MERGED = (BLK, PANELS, TILE, TILE)
LEFT = pltpu.VMEM((4, USED, TILE, TILE), jnp.bfloat16)


def in_vmem(*arrays):
    return tuple(pltpu.with_memory_space_constraint(a, pltpu.VMEM) for a in arrays)


def multiply_own(plan, left, mine, theirs, after):
    return pl.pallas_call(
        own_kernel,
        out_shape=(pltpu.VMEM(EARLY, jnp.float32), pltpu.SMEM((8,), jnp.int32)),
        in_specs=[SMEM] + [VMEM] * 10 + [ANY] * 2,
        out_specs=(VMEM, SMEM),
        scratch_shapes=[LEFT],
        compiler_params=pltpu.CompilerParams(vmem_limit_bytes=LIMIT),
        cost_estimate=pl.CostEstimate(flops=2 * 96 * TILE**3, bytes_accessed=16 << 20, transcendentals=0),
    )(plan, *in_vmem(*left, *mine, *theirs), *after)


def multiply_other(plan, own_left, left, mine, theirs, early, done):
    return pl.pallas_call(
        other_kernel,
        out_shape=(pltpu.VMEM(MERGED, jnp.float32), pltpu.HBM((PANELS, BLK, TILE), jnp.float32)),
        in_specs=[SMEM] + [VMEM] * 17 + [ANY],
        out_specs=(VMEM, VMEM),
        scratch_shapes=[LEFT, LEFT, pltpu.VMEM((BLK, TILE), jnp.float32)],
        compiler_params=pltpu.CompilerParams(vmem_limit_bytes=LIMIT),
        cost_estimate=pl.CostEstimate(flops=2 * 96 * TILE**3, bytes_accessed=16 << 20, transcendentals=0),
    )(plan, *in_vmem(*own_left, *left, *mine, *theirs, early), token(Y2_COST, *left[1:], done))


def scale_kernel(plan, merged, totals, out, factor):
    d = pl.program_id(0)
    pair = plan[END] // 2

    @pl.when(d == 0)
    def _():
        factor[...] = float(PANELS * PANELS * TILE) / (jnp.sum(totals[...], axis=0) + 1e-6)

    def step(n, carry):
        for u in range(GROUP):
            t = n * GROUP + u
            scaling = factor[pl.ds(t, 1), :]
            for half in range(2):
                tile = merged[t, plan[MERGE + (half * 4 + d) * BLK + t]]
                out[pair if half == 0 else 1 - pair, t] = (tile * tile * scaling).astype(jnp.bfloat16)
        return carry

    lax.fori_loop(0, BLK // GROUP, step, 0)


def scale(plan, merged, totals):
    def place(d, plan):
        away = jnp.where(d == 1, 3, jnp.where(d == 2, 1, jnp.where(d == 3, 2, 0)))
        return (plan[END + 2] + away) % 4, 0, 0, 0

    return pl.pallas_call(
        scale_kernel,
        out_shape=jax.ShapeDtypeStruct((PANELS, BLK, TILE, TILE), jnp.bfloat16),
        grid_spec=pltpu.PrefetchScalarGridSpec(
            num_scalar_prefetch=1,
            grid=(4,),
            in_specs=[VMEM, VMEM],
            out_specs=pl.BlockSpec((2, BLK, TILE, TILE), place),
            scratch_shapes=[pltpu.VMEM((BLK, TILE), jnp.float32)],
        ),
        compiler_params=pltpu.CompilerParams(vmem_limit_bytes=LIMIT),
        cost_estimate=pl.CostEstimate(flops=2 * 192 * TILE**2, bytes_accessed=20 << 20, transcendentals=0),
    )(plan, *in_vmem(merged), totals)


def exchange(send):
    return (send[0],) + tuple(lax.ppermute(part, "y", way) for part, way in zip(send[1:], (UP, ACROSS, DOWN)))


def on_device(tile_values, tile_rows):
    own = tile_values[0]
    pos = jnp.stack([lax.axis_index(a) for a in ("x", "y", "z", "core")]).astype(jnp.int32)
    inner = lax.ppermute(own, "x", INNER)
    outer = lax.ppermute(own, "x", OUTER)
    wide_rows = jnp.pad(tile_rows, ((0, 0), (0, TILE - BLK)))
    rows = lax.all_to_all(jnp.broadcast_to(wide_rows, (PANELS, 1, TILE)), ("z", "core"), 0, 0)
    own_rows = jnp.pad(tile_rows, ((0, 0), (OWN_ROWS, TILE - OWN_ROWS - BLK)))
    asks = jnp.broadcast_to(rows.reshape(4, 1, 2, TILE) + own_rows, (4, 4, 2, TILE)).reshape(COLS, 2, TILE)
    req = lax.all_to_all(asks, ("y", "x"), 0, 0)
    own_z, rows_z = lax.optimization_barrier((own, rows))
    below = lax.ppermute(own_z, "z", UP)
    above = lax.ppermute(own_z, "z", DOWN)

    their_own = lax.ppermute(own, "core", SWAP)
    arrived = token(TOKEN_COST, inner, outer, their_own)
    *send1, lists = select_own(pos, req, own, inner, arrived)
    left1 = exchange(send1)
    diag = lax.ppermute(outer, "x", INNER)

    far = lax.ppermute(jnp.where(lax.axis_index("core") == 0, below, above), ("z", "core"), FAR)
    plan = make_plan(pos, rows_z, req, diag)
    sent = pltpu.HBM((USED, TILE, TILE), jnp.bfloat16)
    after = (token(Y1_COST, left1[1]), token(DIAG_COST, diag), lists)
    send2 = select(select_other_kernel, (sent,) * 4, lists, (outer, diag), after)
    left2 = exchange(send2)
    mine = (own, below, above)
    kept, *later = lax.optimization_barrier((send2[0], below, above))
    theirs = (their_own, *(lax.ppermute(block, "core", SWAP) for block in later))
    left2 = (kept, *left2[1:])
    early, done = multiply_own(plan, left1, mine, theirs, (kept, token(Y1_LATE_COST, *left1[2:])))
    kept2, far = lax.optimization_barrier((kept, far))
    left2 = (kept2, *left2[1:])
    mine, theirs = (*mine, far), (*theirs, lax.ppermute(far, "core", SWAP))
    merged, totals = multiply_other(plan, left1, left2, mine, theirs, early, done)
    totals = lax.all_to_all(totals, ("z", "core"), 0, 0)
    return scale(plan, merged, totals)[None]


def solution(mesh):
    fine = Mesh(np.asarray(mesh.devices).reshape(4, 2, 4, 4), ("z", "core", "y", "x"))
    rows, cols = ("z", "core"), ("y", "x")
    return jax.shard_map(
        on_device,
        mesh=fine,
        in_specs=(P(rows, cols, None, None), P(rows, cols)),
        out_specs=P(rows, None, cols, None, None),
        check_vma=False,
    )
```

```python
import jax
import jax.numpy as jnp
import numpy as np
from jax import lax
from jax.experimental import pallas as pl
from jax.experimental.pallas import tpu as pltpu
from jax.sharding import Mesh, PartitionSpec as P

TILE = 128
BLK = 24
USED = 8
PANELS = 8
COLS = 16
GROUP = 4
AT = 10
MERGE = PANELS * BLK
END = 2 * MERGE
OWN_ROWS = 32
LIMIT = 12 << 20
PLAN_COST = 32 << 20
TOKEN_COST = 16
Y1_COST = 0
Y1_LATE_COST = 60
Y2_COST = 20
DIAG_COST = 20
LISTS_COST = 0
DZ = (0, 3, 1, 2)
INNER = [(0, 1), (1, 0), (2, 3), (3, 2)]
OUTER = [(0, 3), (3, 0), (1, 2), (2, 1)]
UP = [(i, (i + 1) % 4) for i in range(4)]
DOWN = [(i, (i + 3) % 4) for i in range(4)]
ACROSS = [(i, (i + 2) % 4) for i in range(4)]
FAR = [(2 * z, 2 * ((z + 1) % 4)) for z in range(4)] + [(2 * z + 1, 2 * ((z + 3) % 4) + 1) for z in range(4)]
SWAP = [(0, 1), (1, 0)]

SMEM = pl.BlockSpec(memory_space=pltpu.SMEM)
VMEM = pl.BlockSpec(memory_space=pltpu.VMEM)
ANY = pl.BlockSpec(memory_space=pl.ANY)


def split_row(row):
    upper = (row >= BLK).astype(jnp.int32)
    return upper, row - upper * BLK


def used_rows(load):
    mask = jnp.int32(0)
    for t in range(BLK):
        upper, local = split_row(load(t))
        mask = mask | lax.shift_left(jnp.int32(1), local)
    return upper, mask


def token_kernel(*refs):
    refs[-1][0] = jnp.int32(0)


def token(cost, *arrays):
    return pl.pallas_call(
        token_kernel,
        out_shape=pltpu.SMEM((8,), jnp.int32),
        in_specs=[ANY] * len(arrays),
        out_specs=SMEM,
        compiler_params=pltpu.CompilerParams(vmem_limit_bytes=1 << 20),
        cost_estimate=pl.CostEstimate(flops=cost * 10**9, bytes_accessed=0, transcendentals=0),
    )(*arrays)


def bit(mask, v):
    return lax.shift_right_logical(mask, jnp.int32(v)) & 1


def lists_kernel(pos, req, lists):
    for pair in range(2):
        for dest in range(4):
            base = (pair * 4 + dest) * 16
            upper, mask = used_rows(lambda t: req[dest * 4 + pos[0], pair, t])
            count = jnp.int32(0)
            for v in range(BLK):
                lists[base + count] = jnp.int32(v)
                count = count + bit(mask, v)
            lists[base + 15] = upper
    for n in range(4):
        lists[AT + n] = pos[n]


def select_own_kernel(pos, req, own, inner, _, *refs):
    outs, lists = refs[:4], refs[4]
    lists_kernel(pos, req, lists)
    pair = lists[AT] // 2
    side = lists[AT] % 2
    for away in range(4):
        base = (pair * 4 + (lists[AT + 1] + away) % 4) * 16
        upper = lists[base + 15]

        def copy(source, out=outs[away], base=base):
            for n in range(USED):
                out[n] = source[lists[base + n]]

        pl.when(upper == side)(lambda: copy(own))
        pl.when(upper != side)(lambda: copy(inner))


def select_other_kernel(lists, outer, diag, _, __, ___, *outs):
    pair = 1 - lists[AT] // 2
    side = (3 - lists[AT]) % 2
    for away in range(4):
        base = (pair * 4 + (lists[AT + 1] + away) % 4) * 16
        upper = lists[base + 15]

        def copy(source, out=outs[away], base=base):
            for n in range(USED):
                out[n] = source[lists[base + n]]

        pl.when(upper == side)(lambda: copy(outer))
        pl.when(upper != side)(lambda: copy(diag))


def select_own(pos, req, own, inner, after):
    return pl.pallas_call(
        select_own_kernel,
        out_shape=(pltpu.HBM((USED, TILE, TILE), jnp.bfloat16),) * 4 + (pltpu.SMEM((128,), jnp.int32),),
        in_specs=[SMEM, SMEM, VMEM, VMEM, ANY],
        out_specs=(VMEM,) * 4 + (SMEM,),
        compiler_params=pltpu.CompilerParams(vmem_limit_bytes=8 << 20),
        cost_estimate=pl.CostEstimate(flops=0, bytes_accessed=2 << 20, transcendentals=0),
    )(pos, req, own, inner, after)


def select(kernel, out_shape, lists, blocks, after):
    return pl.pallas_call(
        kernel,
        out_shape=out_shape,
        in_specs=[SMEM] + [VMEM] * len(blocks) + [ANY] * len(after),
        out_specs=jax.tree.map(lambda _: VMEM, out_shape),
        compiler_params=pltpu.CompilerParams(vmem_limit_bytes=8 << 20),
        cost_estimate=pl.CostEstimate(flops=0, bytes_accessed=2 << 20, transcendentals=0),
    )(lists, *blocks, *after)


def panel_of(pos, at, j):
    z = (pos[at + 2] + DZ[j % 4]) % 4
    pair = pos[at] // 2
    return z, 2 * z + (pair if j < 4 else 1 - pair)


def plan_kernel(pos, rows, req, _, plan, rank):
    uppers = []
    sources = []
    for j in range(PANELS):
        z, panel = panel_of(pos, 0, j)
        upper, mask = used_rows(lambda t: rows[panel, 0, t])
        uppers.append(upper)
        sources.append(z * 4 + 2 * (panel % 2) + upper)
        count = jnp.int32(0)
        for v in range(BLK):
            rank[j * BLK + v] = count
            count = count + bit(mask, v)

    def step(t, carry):
        out_rows = []
        for j in range(PANELS):
            _, panel = panel_of(pos, 0, j)
            local = rows[panel, 0, t] - uppers[j] * BLK
            plan[j * BLK + t] = rank[j * BLK + local]
            out_row = req[sources[j], 0, OWN_ROWS + local]
            place = jnp.int32(j)
            for earlier in reversed(range(j)):
                place = jnp.where(out_rows[earlier] == out_row, earlier, place)
            out_rows.append(out_row)
            plan[MERGE + j * BLK + t] = place
        return carry

    lax.fori_loop(0, BLK, step, 0)
    for n in range(4):
        plan[END + n] = pos[n]


def make_plan(pos, rows, req, after):
    return pl.pallas_call(
        plan_kernel,
        out_shape=pltpu.SMEM((512,), jnp.int32),
        in_specs=[SMEM] * 3 + [ANY],
        out_specs=SMEM,
        scratch_shapes=[pltpu.SMEM((PANELS * BLK,), jnp.int32)],
        compiler_params=pltpu.CompilerParams(vmem_limit_bytes=1 << 20),
        cost_estimate=pl.CostEstimate(flops=0, bytes_accessed=PLAN_COST, transcendentals=0),
    )(pos, rows, req, after)


def products(plan, left, rights, places, n, put):
    for u in range(GROUP):
        t = n * GROUP + u
        for j in places:
            z, _ = panel_of(plan, END, j)
            product = jnp.dot(left[z, plan[j * BLK + t]], rights[j % 4][t], preferred_element_type=jnp.float32)
            put(t, j, product)


def run_both(plan, mine, theirs, work):
    same = plan[END] // 2 == plan[END + 3]
    pl.when(same)(lambda: work(mine, theirs))
    pl.when(jnp.logical_not(same))(lambda: work(theirs, mine))


def gather(plan, pieces, left):
    for away, piece in enumerate(pieces):
        left[(plan[END + 1] - away) % 4] = piece[...]


def own_kernel(plan, *refs):
    pieces, mine, theirs, (_, _, early, done, left) = refs[:4], refs[4:7], refs[7:10], refs[10:]
    done[0] = jnp.int32(0)
    gather(plan, pieces, left)

    def work(rights, _):
        def step(n, carry):
            def put(t, j, product):
                if j == 0:
                    early[t, 0] = product
                else:
                    r = plan[MERGE + j * BLK + t]
                    early[t, r] = jnp.where(r == j, 0.0, early[t, r]) + product

            products(plan, left, rights, range(3), n, put)
            return carry

        lax.fori_loop(0, BLK // GROUP, step, 0)

    run_both(plan, mine, theirs, work)


def other_kernel(plan, *refs):
    own_pieces, pieces, mine, theirs = refs[:4], refs[4:8], refs[8:12], refs[12:16]
    early, _, merged, totals, own_left, left, sums = refs[16:]
    gather(plan, own_pieces, own_left)
    gather(plan, pieces, left)

    def add_up(n):
        for u in range(GROUP):
            t = n * GROUP + u
            total = jnp.zeros((8, TILE), jnp.float32)
            for j in range(PANELS):
                tile = merged[t, j]
                part = jnp.sum((tile * tile).reshape(16, 8, TILE), axis=0)
                total = total + jnp.where(plan[MERGE + j * BLK + t] == j, part, 0.0)
            sums[pl.ds(t, 1), :] = jnp.sum(total, axis=0, keepdims=True)

    def work(own_rights, rights):
        def step(n, carry):
            def put(t, j, product):
                r = plan[MERGE + j * BLK + t]
                merged[t, r] = jnp.where(r == j, 0.0, merged[t, r]) + product

            for u in range(GROUP):
                for j in range(3):
                    merged[n * GROUP + u, j] = early[n * GROUP + u, j]
            products(plan, own_left, own_rights, (3,), n, put)
            products(plan, left, rights, range(4, PANELS), n, put)
            add_up(jnp.maximum(n - 1, 0))
            return carry

        lax.fori_loop(0, BLK // GROUP, step, 0)

    run_both(plan, mine, theirs, work)
    add_up(BLK // GROUP - 1)
    for i in range(PANELS):
        totals[i] = sums[...]


EARLY = (BLK, 3, TILE, TILE)
MERGED = (BLK, PANELS, TILE, TILE)
LEFT = pltpu.VMEM((4, USED, TILE, TILE), jnp.bfloat16)


def in_vmem(*arrays):
    return tuple(pltpu.with_memory_space_constraint(a, pltpu.VMEM) for a in arrays)


def multiply_own(plan, left, mine, theirs, after):
    return pl.pallas_call(
        own_kernel,
        out_shape=(pltpu.VMEM(EARLY, jnp.float32), pltpu.SMEM((8,), jnp.int32)),
        in_specs=[SMEM] + [VMEM] * 10 + [ANY] * 2,
        out_specs=(VMEM, SMEM),
        scratch_shapes=[LEFT],
        compiler_params=pltpu.CompilerParams(vmem_limit_bytes=LIMIT),
        cost_estimate=pl.CostEstimate(flops=2 * 96 * TILE**3, bytes_accessed=16 << 20, transcendentals=0),
    )(plan, *in_vmem(*left, *mine, *theirs), *after)


def multiply_other(plan, own_left, left, mine, theirs, early, done):
    return pl.pallas_call(
        other_kernel,
        out_shape=(pltpu.VMEM(MERGED, jnp.float32), pltpu.HBM((PANELS, BLK, TILE), jnp.float32)),
        in_specs=[SMEM] + [VMEM] * 17 + [ANY],
        out_specs=(VMEM, VMEM),
        scratch_shapes=[LEFT, LEFT, pltpu.VMEM((BLK, TILE), jnp.float32)],
        compiler_params=pltpu.CompilerParams(vmem_limit_bytes=LIMIT),
        cost_estimate=pl.CostEstimate(flops=2 * 96 * TILE**3, bytes_accessed=16 << 20, transcendentals=0),
    )(plan, *in_vmem(*own_left, *left, *mine, *theirs, early), token(Y2_COST, *left[1:], done))


def scale_kernel(plan, merged, totals, out, factor):
    d = pl.program_id(0)
    pair = plan[END] // 2

    @pl.when(d == 0)
    def _():
        factor[...] = float(PANELS * PANELS * TILE) / (jnp.sum(totals[...], axis=0) + 1e-6)

    def step(n, carry):
        for u in range(GROUP):
            t = n * GROUP + u
            scaling = factor[pl.ds(t, 1), :]
            for half in range(2):
                tile = merged[t, plan[MERGE + (half * 4 + d) * BLK + t]]
                out[pair if half == 0 else 1 - pair, t] = (tile * tile * scaling).astype(jnp.bfloat16)
        return carry

    lax.fori_loop(0, BLK // GROUP, step, 0)


def scale(plan, merged, totals):
    def place(d, plan):
        away = jnp.where(d == 1, 3, jnp.where(d == 2, 1, jnp.where(d == 3, 2, 0)))
        return (plan[END + 2] + away) % 4, 0, 0, 0

    return pl.pallas_call(
        scale_kernel,
        out_shape=jax.ShapeDtypeStruct((PANELS, BLK, TILE, TILE), jnp.bfloat16),
        grid_spec=pltpu.PrefetchScalarGridSpec(
            num_scalar_prefetch=1,
            grid=(4,),
            in_specs=[VMEM, VMEM],
            out_specs=pl.BlockSpec((2, BLK, TILE, TILE), place),
            scratch_shapes=[pltpu.VMEM((BLK, TILE), jnp.float32)],
        ),
        compiler_params=pltpu.CompilerParams(vmem_limit_bytes=LIMIT),
        cost_estimate=pl.CostEstimate(flops=2 * 192 * TILE**2, bytes_accessed=20 << 20, transcendentals=0),
    )(plan, *in_vmem(merged), totals)


def exchange(send):
    return (send[0],) + tuple(lax.ppermute(part, "y", way) for part, way in zip(send[1:], (UP, ACROSS, DOWN)))


def on_device(tile_values, tile_rows):
    own = tile_values[0]
    pos = jnp.stack([lax.axis_index(a) for a in ("x", "y", "z", "core")]).astype(jnp.int32)
    inner = lax.ppermute(own, "x", INNER)
    outer = lax.ppermute(own, "x", OUTER)
    wide_rows = jnp.pad(tile_rows, ((0, 0), (0, TILE - BLK)))
    rows = lax.all_to_all(jnp.broadcast_to(wide_rows, (PANELS, 1, TILE)), ("z", "core"), 0, 0)
    own_rows = jnp.pad(tile_rows, ((0, 0), (OWN_ROWS, TILE - OWN_ROWS - BLK)))
    asks = jnp.broadcast_to(rows.reshape(4, 1, 2, TILE) + own_rows, (4, 4, 2, TILE)).reshape(COLS, 2, TILE)
    req = lax.all_to_all(asks, ("y", "x"), 0, 0)
    own_z, rows_z = lax.optimization_barrier((own, rows))
    below = lax.ppermute(own_z, "z", UP)
    above = lax.ppermute(own_z, "z", DOWN)

    their_own = lax.ppermute(own, "core", SWAP)
    arrived = token(TOKEN_COST, inner, outer, their_own)
    *send1, lists = select_own(pos, req, own, inner, arrived)
    left1 = exchange(send1)
    diag = lax.ppermute(outer, "x", INNER)

    far = lax.ppermute(jnp.where(lax.axis_index("core") == 0, below, above), ("z", "core"), FAR)
    plan = make_plan(pos, rows_z, req, diag)
    sent = pltpu.HBM((USED, TILE, TILE), jnp.bfloat16)
    after = (lists, token(DIAG_COST, diag), lists)
    send2 = select(select_other_kernel, (sent,) * 4, lists, (outer, diag), after)
    left2 = exchange(send2)
    mine = (own, below, above)
    kept, *later = lax.optimization_barrier((send2[0], below, above))
    theirs = (their_own, *(lax.ppermute(block, "core", SWAP) for block in later))
    left2 = (kept, *left2[1:])
    early, done = multiply_own(plan, left1, mine, theirs, (kept, token(Y1_LATE_COST, *left1[1:])))
    kept2, far = lax.optimization_barrier((kept, far))
    left2 = (kept2, *left2[1:])
    mine, theirs = (*mine, far), (*theirs, lax.ppermute(far, "core", SWAP))
    merged, totals = multiply_other(plan, left1, left2, mine, theirs, early, done)
    totals = lax.all_to_all(totals, ("z", "core"), 0, 0)
    return scale(plan, merged, totals)[None]


def solution(mesh):
    fine = Mesh(np.asarray(mesh.devices).reshape(4, 2, 4, 4), ("z", "core", "y", "x"))
    rows, cols = ("z", "core"), ("y", "x")
    return jax.shard_map(
        on_device,
        mesh=fine,
        in_specs=(P(rows, cols, None, None), P(rows, cols)),
        out_specs=P(rows, None, cols, None, None),
        check_vma=False,
    )
```

```python
import jax
import jax.numpy as jnp
import numpy as np
from jax import lax
from jax.experimental import pallas as pl
from jax.experimental.pallas import tpu as pltpu
from jax.sharding import Mesh, PartitionSpec as P

TILE = 128
BLK = 24
USED = 8
PANELS = 8
COLS = 16
GROUP = 4
AT = 10
MERGE = PANELS * BLK
END = 2 * MERGE
OWN_ROWS = 32
LIMIT = 12 << 20
PLAN_COST = 32 << 20
TOKEN_COST = 16
Y1_COST = 0
Y1_LATE_COST = 60
Y2_COST = 20
DIAG_COST = 20
LISTS_COST = 0
DZ = (0, 3, 1, 2)
INNER = [(0, 1), (1, 0), (2, 3), (3, 2)]
OUTER = [(0, 3), (3, 0), (1, 2), (2, 1)]
UP = [(i, (i + 1) % 4) for i in range(4)]
DOWN = [(i, (i + 3) % 4) for i in range(4)]
ACROSS = [(i, (i + 2) % 4) for i in range(4)]
FAR = [(2 * z, 2 * ((z + 1) % 4)) for z in range(4)] + [(2 * z + 1, 2 * ((z + 3) % 4) + 1) for z in range(4)]
SWAP = [(0, 1), (1, 0)]

SMEM = pl.BlockSpec(memory_space=pltpu.SMEM)
VMEM = pl.BlockSpec(memory_space=pltpu.VMEM)
ANY = pl.BlockSpec(memory_space=pl.ANY)


def split_row(row):
    upper = (row >= BLK).astype(jnp.int32)
    return upper, row - upper * BLK


def used_rows(load):
    mask = jnp.int32(0)
    for t in range(BLK):
        upper, local = split_row(load(t))
        mask = mask | lax.shift_left(jnp.int32(1), local)
    return upper, mask


def token_kernel(*refs):
    refs[-1][0] = jnp.int32(0)


def token(cost, *arrays):
    return pl.pallas_call(
        token_kernel,
        out_shape=pltpu.SMEM((8,), jnp.int32),
        in_specs=[ANY] * len(arrays),
        out_specs=SMEM,
        compiler_params=pltpu.CompilerParams(vmem_limit_bytes=1 << 20),
        cost_estimate=pl.CostEstimate(flops=cost * 10**9, bytes_accessed=0, transcendentals=0),
    )(*arrays)


def bring_kernel(source, _, out, flag, sem):
    copy = pltpu.make_async_copy(source, out, sem)
    copy.start()
    copy.wait()
    flag[0] = jnp.int32(0)


def bring(block, after):
    return pl.pallas_call(
        bring_kernel,
        out_shape=(pltpu.VMEM(block.shape, block.dtype), pltpu.SMEM((8,), jnp.int32)),
        in_specs=[ANY, ANY],
        out_specs=(VMEM, SMEM),
        scratch_shapes=[pltpu.SemaphoreType.DMA],
        compiler_params=pltpu.CompilerParams(vmem_limit_bytes=2 << 20),
        cost_estimate=pl.CostEstimate(flops=0, bytes_accessed=2 << 20, transcendentals=0),
    )(block, after)


def bit(mask, v):
    return lax.shift_right_logical(mask, jnp.int32(v)) & 1


def lists_kernel(pos, req, lists):
    for pair in range(2):
        for dest in range(4):
            base = (pair * 4 + dest) * 16
            upper, mask = used_rows(lambda t: req[dest * 4 + pos[0], pair, t])
            count = jnp.int32(0)
            for v in range(BLK):
                lists[base + count] = jnp.int32(v)
                count = count + bit(mask, v)
            lists[base + 15] = upper
    for n in range(4):
        lists[AT + n] = pos[n]


def select_own_kernel(pos, req, own, inner, _, *refs):
    outs, lists = refs[:4], refs[4]
    lists_kernel(pos, req, lists)
    pair = lists[AT] // 2
    side = lists[AT] % 2
    for away in range(4):
        base = (pair * 4 + (lists[AT + 1] + away) % 4) * 16
        upper = lists[base + 15]

        def copy(source, out=outs[away], base=base):
            for n in range(USED):
                out[n] = source[lists[base + n]]

        pl.when(upper == side)(lambda: copy(own))
        pl.when(upper != side)(lambda: copy(inner))


def select_other_kernel(lists, outer, diag, _, __, ___, *outs):
    pair = 1 - lists[AT] // 2
    side = (3 - lists[AT]) % 2
    for away in range(4):
        base = (pair * 4 + (lists[AT + 1] + away) % 4) * 16
        upper = lists[base + 15]

        def copy(source, out=outs[away], base=base):
            for n in range(USED):
                out[n] = source[lists[base + n]]

        pl.when(upper == side)(lambda: copy(outer))
        pl.when(upper != side)(lambda: copy(diag))


def select_own(pos, req, own, inner, after):
    return pl.pallas_call(
        select_own_kernel,
        out_shape=(pltpu.HBM((USED, TILE, TILE), jnp.bfloat16),) * 4 + (pltpu.SMEM((128,), jnp.int32),),
        in_specs=[SMEM, SMEM, VMEM, VMEM, ANY],
        out_specs=(VMEM,) * 4 + (SMEM,),
        compiler_params=pltpu.CompilerParams(vmem_limit_bytes=8 << 20),
        cost_estimate=pl.CostEstimate(flops=0, bytes_accessed=2 << 20, transcendentals=0),
    )(pos, req, own, inner, after)


def select(kernel, out_shape, lists, blocks, after):
    return pl.pallas_call(
        kernel,
        out_shape=out_shape,
        in_specs=[SMEM] + [VMEM] * len(blocks) + [ANY] * len(after),
        out_specs=jax.tree.map(lambda _: VMEM, out_shape),
        compiler_params=pltpu.CompilerParams(vmem_limit_bytes=8 << 20),
        cost_estimate=pl.CostEstimate(flops=0, bytes_accessed=2 << 20, transcendentals=0),
    )(lists, *blocks, *after)


def panel_of(pos, at, j):
    z = (pos[at + 2] + DZ[j % 4]) % 4
    pair = pos[at] // 2
    return z, 2 * z + (pair if j < 4 else 1 - pair)


def plan_kernel(pos, rows, req, _, plan, rank):
    uppers = []
    sources = []
    for j in range(PANELS):
        z, panel = panel_of(pos, 0, j)
        upper, mask = used_rows(lambda t: rows[panel, 0, t])
        uppers.append(upper)
        sources.append(z * 4 + 2 * (panel % 2) + upper)
        count = jnp.int32(0)
        for v in range(BLK):
            rank[j * BLK + v] = count
            count = count + bit(mask, v)

    def step(t, carry):
        out_rows = []
        for j in range(PANELS):
            _, panel = panel_of(pos, 0, j)
            local = rows[panel, 0, t] - uppers[j] * BLK
            plan[j * BLK + t] = rank[j * BLK + local]
            out_row = req[sources[j], 0, OWN_ROWS + local]
            place = jnp.int32(j)
            for earlier in reversed(range(j)):
                place = jnp.where(out_rows[earlier] == out_row, earlier, place)
            out_rows.append(out_row)
            plan[MERGE + j * BLK + t] = place
        return carry

    lax.fori_loop(0, BLK, step, 0)
    for n in range(4):
        plan[END + n] = pos[n]


def make_plan(pos, rows, req, after):
    return pl.pallas_call(
        plan_kernel,
        out_shape=pltpu.SMEM((512,), jnp.int32),
        in_specs=[SMEM] * 3 + [ANY],
        out_specs=SMEM,
        scratch_shapes=[pltpu.SMEM((PANELS * BLK,), jnp.int32)],
        compiler_params=pltpu.CompilerParams(vmem_limit_bytes=1 << 20),
        cost_estimate=pl.CostEstimate(flops=0, bytes_accessed=PLAN_COST, transcendentals=0),
    )(pos, rows, req, after)


def products(plan, left, rights, places, n, put):
    for u in range(GROUP):
        t = n * GROUP + u
        for j in places:
            z, _ = panel_of(plan, END, j)
            product = jnp.dot(left[z, plan[j * BLK + t]], rights[j % 4][t], preferred_element_type=jnp.float32)
            put(t, j, product)


def run_both(plan, mine, theirs, work):
    same = plan[END] // 2 == plan[END + 3]
    pl.when(same)(lambda: work(mine, theirs))
    pl.when(jnp.logical_not(same))(lambda: work(theirs, mine))


def gather(plan, pieces, left):
    for away, piece in enumerate(pieces):
        left[(plan[END + 1] - away) % 4] = piece[...]


def own_kernel(plan, *refs):
    pieces, mine, theirs, (_, _, early, done, left) = refs[:4], refs[4:7], refs[7:10], refs[10:]
    done[0] = jnp.int32(0)
    gather(plan, pieces, left)

    def work(rights, _):
        def step(n, carry):
            def put(t, j, product):
                if j == 0:
                    early[t, 0] = product
                else:
                    r = plan[MERGE + j * BLK + t]
                    early[t, r] = jnp.where(r == j, 0.0, early[t, r]) + product

            products(plan, left, rights, range(3), n, put)
            return carry

        lax.fori_loop(0, BLK // GROUP, step, 0)

    run_both(plan, mine, theirs, work)


def other_kernel(plan, *refs):
    own_pieces, pieces, mine, theirs = refs[:4], refs[4:8], refs[8:12], refs[12:16]
    early, _, merged, totals, own_left, left, sums = refs[16:]
    gather(plan, own_pieces, own_left)
    gather(plan, pieces, left)

    def add_up(n):
        for u in range(GROUP):
            t = n * GROUP + u
            total = jnp.zeros((8, TILE), jnp.float32)
            for j in range(PANELS):
                tile = merged[t, j]
                part = jnp.sum((tile * tile).reshape(16, 8, TILE), axis=0)
                total = total + jnp.where(plan[MERGE + j * BLK + t] == j, part, 0.0)
            sums[pl.ds(t, 1), :] = jnp.sum(total, axis=0, keepdims=True)

    def work(own_rights, rights):
        def step(n, carry):
            def put(t, j, product):
                r = plan[MERGE + j * BLK + t]
                merged[t, r] = jnp.where(r == j, 0.0, merged[t, r]) + product

            for u in range(GROUP):
                for j in range(3):
                    merged[n * GROUP + u, j] = early[n * GROUP + u, j]
            products(plan, own_left, own_rights, (3,), n, put)
            products(plan, left, rights, range(4, PANELS), n, put)
            add_up(jnp.maximum(n - 1, 0))
            return carry

        lax.fori_loop(0, BLK // GROUP, step, 0)

    run_both(plan, mine, theirs, work)
    add_up(BLK // GROUP - 1)
    for i in range(PANELS):
        totals[i] = sums[...]


EARLY = (BLK, 3, TILE, TILE)
MERGED = (BLK, PANELS, TILE, TILE)
LEFT = pltpu.VMEM((4, USED, TILE, TILE), jnp.bfloat16)


def in_vmem(*arrays):
    return tuple(pltpu.with_memory_space_constraint(a, pltpu.VMEM) for a in arrays)


def multiply_own(plan, left, mine, theirs, after):
    return pl.pallas_call(
        own_kernel,
        out_shape=(pltpu.VMEM(EARLY, jnp.float32), pltpu.SMEM((8,), jnp.int32)),
        in_specs=[SMEM] + [VMEM] * 10 + [ANY] * 2,
        out_specs=(VMEM, SMEM),
        scratch_shapes=[LEFT],
        compiler_params=pltpu.CompilerParams(vmem_limit_bytes=LIMIT),
        cost_estimate=pl.CostEstimate(flops=2 * 96 * TILE**3, bytes_accessed=16 << 20, transcendentals=0),
    )(plan, *in_vmem(*left, *mine, *theirs), *after)


def multiply_other(plan, own_left, left, mine, theirs, early, done):
    return pl.pallas_call(
        other_kernel,
        out_shape=(pltpu.VMEM(MERGED, jnp.float32), pltpu.HBM((PANELS, BLK, TILE), jnp.float32)),
        in_specs=[SMEM] + [VMEM] * 17 + [ANY],
        out_specs=(VMEM, VMEM),
        scratch_shapes=[LEFT, LEFT, pltpu.VMEM((BLK, TILE), jnp.float32)],
        compiler_params=pltpu.CompilerParams(vmem_limit_bytes=LIMIT),
        cost_estimate=pl.CostEstimate(flops=2 * 96 * TILE**3, bytes_accessed=16 << 20, transcendentals=0),
    )(plan, *in_vmem(*own_left, *left, *mine, *theirs, early), token(Y2_COST, *left[1:], done))


def scale_kernel(plan, merged, totals, out, factor):
    d = pl.program_id(0)
    pair = plan[END] // 2

    @pl.when(d == 0)
    def _():
        factor[...] = float(PANELS * PANELS * TILE) / (jnp.sum(totals[...], axis=0) + 1e-6)

    def step(n, carry):
        for u in range(GROUP):
            t = n * GROUP + u
            scaling = factor[pl.ds(t, 1), :]
            for half in range(2):
                tile = merged[t, plan[MERGE + (half * 4 + d) * BLK + t]]
                out[pair if half == 0 else 1 - pair, t] = (tile * tile * scaling).astype(jnp.bfloat16)
        return carry

    lax.fori_loop(0, BLK // GROUP, step, 0)


def scale(plan, merged, totals):
    def place(d, plan):
        away = jnp.where(d == 1, 3, jnp.where(d == 2, 1, jnp.where(d == 3, 2, 0)))
        return (plan[END + 2] + away) % 4, 0, 0, 0

    return pl.pallas_call(
        scale_kernel,
        out_shape=jax.ShapeDtypeStruct((PANELS, BLK, TILE, TILE), jnp.bfloat16),
        grid_spec=pltpu.PrefetchScalarGridSpec(
            num_scalar_prefetch=1,
            grid=(4,),
            in_specs=[VMEM, VMEM],
            out_specs=pl.BlockSpec((2, BLK, TILE, TILE), place),
            scratch_shapes=[pltpu.VMEM((BLK, TILE), jnp.float32)],
        ),
        compiler_params=pltpu.CompilerParams(vmem_limit_bytes=LIMIT),
        cost_estimate=pl.CostEstimate(flops=2 * 192 * TILE**2, bytes_accessed=20 << 20, transcendentals=0),
    )(plan, *in_vmem(merged), totals)


def exchange(send):
    return (send[0],) + tuple(lax.ppermute(part, "y", way) for part, way in zip(send[1:], (UP, ACROSS, DOWN)))


def on_device(tile_values, tile_rows):
    own = tile_values[0]
    pos = jnp.stack([lax.axis_index(a) for a in ("x", "y", "z", "core")]).astype(jnp.int32)
    inner = lax.ppermute(own, "x", INNER)
    outer = lax.ppermute(own, "x", OUTER)
    wide_rows = jnp.pad(tile_rows, ((0, 0), (0, TILE - BLK)))
    rows = lax.all_to_all(jnp.broadcast_to(wide_rows, (PANELS, 1, TILE)), ("z", "core"), 0, 0)
    own_rows = jnp.pad(tile_rows, ((0, 0), (OWN_ROWS, TILE - OWN_ROWS - BLK)))
    asks = jnp.broadcast_to(rows.reshape(4, 1, 2, TILE) + own_rows, (4, 4, 2, TILE)).reshape(COLS, 2, TILE)
    req = lax.all_to_all(asks, ("y", "x"), 0, 0)
    own_z, rows_z = lax.optimization_barrier((own, rows))
    below = lax.ppermute(own_z, "z", UP)
    above = lax.ppermute(own_z, "z", DOWN)

    their_own = lax.ppermute(own, "core", SWAP)
    arrived = token(TOKEN_COST, inner, outer, their_own)
    *send1, lists = select_own(pos, req, own, inner, arrived)
    left1 = exchange(send1)
    diag = lax.ppermute(outer, "x", INNER)

    far = lax.ppermute(jnp.where(lax.axis_index("core") == 0, below, above), ("z", "core"), FAR)
    plan = make_plan(pos, rows_z, req, diag)
    sent = pltpu.HBM((USED, TILE, TILE), jnp.bfloat16)
    their_own, brought = bring(their_own, send1[0])
    after = (brought, token(DIAG_COST, diag), lists)
    send2 = select(select_other_kernel, (sent,) * 4, lists, (outer, diag), after)
    left2 = exchange(send2)
    mine = (own, below, above)
    kept, *later = lax.optimization_barrier((send2[0], below, above))
    theirs = (their_own, *(lax.ppermute(block, "core", SWAP) for block in later))
    left2 = (kept, *left2[1:])
    early, done = multiply_own(plan, left1, mine, theirs, (kept, token(Y1_LATE_COST, *left1[1:])))
    kept2, far = lax.optimization_barrier((kept, far))
    left2 = (kept2, *left2[1:])
    mine, theirs = (*mine, far), (*theirs, lax.ppermute(far, "core", SWAP))
    merged, totals = multiply_other(plan, left1, left2, mine, theirs, early, done)
    totals = lax.all_to_all(totals, ("z", "core"), 0, 0)
    return scale(plan, merged, totals)[None]


def solution(mesh):
    fine = Mesh(np.asarray(mesh.devices).reshape(4, 2, 4, 4), ("z", "core", "y", "x"))
    rows, cols = ("z", "core"), ("y", "x")
    return jax.shard_map(
        on_device,
        mesh=fine,
        in_specs=(P(rows, cols, None, None), P(rows, cols)),
        out_specs=P(rows, None, cols, None, None),
        check_vma=False,
    )
```

```python
import jax
import jax.numpy as jnp
import numpy as np
from jax import lax
from jax.experimental import pallas as pl
from jax.experimental.pallas import tpu as pltpu
from jax.sharding import Mesh, PartitionSpec as P

TILE = 128
BLK = 24
USED = 8
PANELS = 8
COLS = 16
GROUP = 4
AT = 10
MERGE = PANELS * BLK
END = 2 * MERGE
OWN_ROWS = 32
LIMIT = 12 << 20
PLAN_COST = 32 << 20
TOKEN_COST = 16
Y1_COST = 0
Y1_LATE_COST = 60
Y2_COST = 20
DIAG_COST = 20
LISTS_COST = 0
DZ = (0, 3, 1, 2)
INNER = [(0, 1), (1, 0), (2, 3), (3, 2)]
OUTER = [(0, 3), (3, 0), (1, 2), (2, 1)]
UP = [(i, (i + 1) % 4) for i in range(4)]
DOWN = [(i, (i + 3) % 4) for i in range(4)]
ACROSS = [(i, (i + 2) % 4) for i in range(4)]
FAR = [(2 * z, 2 * ((z + 1) % 4)) for z in range(4)] + [(2 * z + 1, 2 * ((z + 3) % 4) + 1) for z in range(4)]
SWAP = [(0, 1), (1, 0)]

SMEM = pl.BlockSpec(memory_space=pltpu.SMEM)
VMEM = pl.BlockSpec(memory_space=pltpu.VMEM)
ANY = pl.BlockSpec(memory_space=pl.ANY)


def split_row(row):
    upper = (row >= BLK).astype(jnp.int32)
    return upper, row - upper * BLK


def used_rows(load):
    mask = jnp.int32(0)
    for t in range(BLK):
        upper, local = split_row(load(t))
        mask = mask | lax.shift_left(jnp.int32(1), local)
    return upper, mask


def token_kernel(*refs):
    refs[-1][0] = jnp.int32(0)


def token(cost, *arrays):
    return pl.pallas_call(
        token_kernel,
        out_shape=pltpu.SMEM((8,), jnp.int32),
        in_specs=[ANY] * len(arrays),
        out_specs=SMEM,
        compiler_params=pltpu.CompilerParams(vmem_limit_bytes=1 << 20),
        cost_estimate=pl.CostEstimate(flops=cost * 10**9, bytes_accessed=0, transcendentals=0),
    )(*arrays)


def bring_kernel(source, _, out, flag, sem):
    copy = pltpu.make_async_copy(source, out, sem)
    copy.start()
    copy.wait()
    flag[0] = jnp.int32(0)


def bring(block, after):
    return pl.pallas_call(
        bring_kernel,
        out_shape=(pltpu.VMEM(block.shape, block.dtype), pltpu.SMEM((8,), jnp.int32)),
        in_specs=[ANY, ANY],
        out_specs=(VMEM, SMEM),
        scratch_shapes=[pltpu.SemaphoreType.DMA],
        compiler_params=pltpu.CompilerParams(vmem_limit_bytes=2 << 20),
        cost_estimate=pl.CostEstimate(flops=0, bytes_accessed=2 << 20, transcendentals=0),
    )(block, after)


def bit(mask, v):
    return lax.shift_right_logical(mask, jnp.int32(v)) & 1


def lists_kernel(pos, req, lists):
    for pair in range(2):
        for dest in range(4):
            base = (pair * 4 + dest) * 16
            upper, mask = used_rows(lambda t: req[dest * 4 + pos[0], pair, t])
            count = jnp.int32(0)
            for v in range(BLK):
                lists[base + count] = jnp.int32(v)
                count = count + bit(mask, v)
            lists[base + 15] = upper
    for n in range(4):
        lists[AT + n] = pos[n]


def select_own_kernel(pos, req, own, inner, _, *refs):
    outs, lists = refs[:4], refs[4]
    lists_kernel(pos, req, lists)
    pair = lists[AT] // 2
    side = lists[AT] % 2
    for away in range(4):
        base = (pair * 4 + (lists[AT + 1] + away) % 4) * 16
        upper = lists[base + 15]

        def copy(source, out=outs[away], base=base):
            for n in range(USED):
                out[n] = source[lists[base + n]]

        pl.when(upper == side)(lambda: copy(own))
        pl.when(upper != side)(lambda: copy(inner))


def select_other_kernel(lists, outer, diag, _, __, ___, *outs):
    pair = 1 - lists[AT] // 2
    side = (3 - lists[AT]) % 2
    for away in range(4):
        base = (pair * 4 + (lists[AT + 1] + away) % 4) * 16
        upper = lists[base + 15]

        def copy(source, out=outs[away], base=base):
            for n in range(USED):
                out[n] = source[lists[base + n]]

        pl.when(upper == side)(lambda: copy(outer))
        pl.when(upper != side)(lambda: copy(diag))


def select_own(pos, req, own, inner, after):
    return pl.pallas_call(
        select_own_kernel,
        out_shape=(pltpu.HBM((USED, TILE, TILE), jnp.bfloat16),) * 4 + (pltpu.SMEM((128,), jnp.int32),),
        in_specs=[SMEM, SMEM, VMEM, VMEM, ANY],
        out_specs=(VMEM,) * 4 + (SMEM,),
        compiler_params=pltpu.CompilerParams(vmem_limit_bytes=8 << 20),
        cost_estimate=pl.CostEstimate(flops=0, bytes_accessed=2 << 20, transcendentals=0),
    )(pos, req, own, inner, after)


def select(kernel, out_shape, lists, blocks, after):
    return pl.pallas_call(
        kernel,
        out_shape=out_shape,
        in_specs=[SMEM] + [VMEM] * len(blocks) + [ANY] * len(after),
        out_specs=jax.tree.map(lambda _: VMEM, out_shape),
        compiler_params=pltpu.CompilerParams(vmem_limit_bytes=8 << 20),
        cost_estimate=pl.CostEstimate(flops=0, bytes_accessed=2 << 20, transcendentals=0),
    )(lists, *blocks, *after)


def panel_of(pos, at, j):
    z = (pos[at + 2] + DZ[j % 4]) % 4
    pair = pos[at] // 2
    return z, 2 * z + (pair if j < 4 else 1 - pair)


def plan_kernel(pos, rows, req, _, plan, rank):
    uppers = []
    sources = []
    for j in range(PANELS):
        z, panel = panel_of(pos, 0, j)
        upper, mask = used_rows(lambda t: rows[panel, 0, t])
        uppers.append(upper)
        sources.append(z * 4 + 2 * (panel % 2) + upper)
        count = jnp.int32(0)
        for v in range(BLK):
            rank[j * BLK + v] = count
            count = count + bit(mask, v)

    def step(t, carry):
        out_rows = []
        for j in range(PANELS):
            _, panel = panel_of(pos, 0, j)
            local = rows[panel, 0, t] - uppers[j] * BLK
            plan[j * BLK + t] = rank[j * BLK + local]
            out_row = req[sources[j], 0, OWN_ROWS + local]
            place = jnp.int32(j)
            for earlier in reversed(range(j)):
                place = jnp.where(out_rows[earlier] == out_row, earlier, place)
            out_rows.append(out_row)
            plan[MERGE + j * BLK + t] = place
        return carry

    lax.fori_loop(0, BLK, step, 0)
    for n in range(4):
        plan[END + n] = pos[n]


def make_plan(pos, rows, req, after):
    return pl.pallas_call(
        plan_kernel,
        out_shape=pltpu.SMEM((512,), jnp.int32),
        in_specs=[SMEM] * 3 + [ANY],
        out_specs=SMEM,
        scratch_shapes=[pltpu.SMEM((PANELS * BLK,), jnp.int32)],
        compiler_params=pltpu.CompilerParams(vmem_limit_bytes=1 << 20),
        cost_estimate=pl.CostEstimate(flops=0, bytes_accessed=PLAN_COST, transcendentals=0),
    )(pos, rows, req, after)


def products(plan, left, rights, places, n, put):
    for u in range(GROUP):
        t = n * GROUP + u
        for j in places:
            z, _ = panel_of(plan, END, j)
            product = jnp.dot(left[z, plan[j * BLK + t]], rights[j % 4][t], preferred_element_type=jnp.float32)
            put(t, j, product)


def run_both(plan, mine, theirs, work):
    same = plan[END] // 2 == plan[END + 3]
    pl.when(same)(lambda: work(mine, theirs))
    pl.when(jnp.logical_not(same))(lambda: work(theirs, mine))


def gather(plan, pieces, left):
    for away, piece in enumerate(pieces):
        left[(plan[END + 1] - away) % 4] = piece[...]


def own_kernel(plan, *refs):
    pieces, mine, theirs, (_, _, early, done, left) = refs[:4], refs[4:7], refs[7:10], refs[10:]
    done[0] = jnp.int32(0)
    gather(plan, pieces, left)

    def work(rights, _):
        def step(n, carry):
            def put(t, j, product):
                if j == 0:
                    early[t, 0] = product
                else:
                    r = plan[MERGE + j * BLK + t]
                    early[t, r] = jnp.where(r == j, 0.0, early[t, r]) + product

            products(plan, left, rights, range(3), n, put)
            return carry

        lax.fori_loop(0, BLK // GROUP, step, 0)

    run_both(plan, mine, theirs, work)


def other_kernel(plan, *refs):
    own_pieces, pieces, mine, theirs = refs[:4], refs[4:8], refs[8:12], refs[12:16]
    early, _, merged, totals, own_left, left, sums = refs[16:]
    gather(plan, own_pieces, own_left)
    gather(plan, pieces, left)

    def add_up(n):
        for u in range(GROUP):
            t = n * GROUP + u
            total = jnp.zeros((8, TILE), jnp.float32)
            for j in range(PANELS):
                tile = merged[t, j]
                part = jnp.sum((tile * tile).reshape(16, 8, TILE), axis=0)
                total = total + jnp.where(plan[MERGE + j * BLK + t] == j, part, 0.0)
            sums[pl.ds(t, 1), :] = jnp.sum(total, axis=0, keepdims=True)

    def work(own_rights, rights):
        def step(n, carry):
            def put(t, j, product):
                r = plan[MERGE + j * BLK + t]
                merged[t, r] = jnp.where(r == j, 0.0, merged[t, r]) + product

            for u in range(GROUP):
                for j in range(3):
                    merged[n * GROUP + u, j] = early[n * GROUP + u, j]
            products(plan, own_left, own_rights, (3,), n, put)
            products(plan, left, rights, range(4, PANELS), n, put)
            add_up(jnp.maximum(n - 1, 0))
            return carry

        lax.fori_loop(0, BLK // GROUP, step, 0)

    run_both(plan, mine, theirs, work)
    add_up(BLK // GROUP - 1)
    for i in range(PANELS):
        totals[i] = sums[...]


EARLY = (BLK, 3, TILE, TILE)
MERGED = (BLK, PANELS, TILE, TILE)
LEFT = pltpu.VMEM((4, USED, TILE, TILE), jnp.bfloat16)


def in_vmem(*arrays):
    return tuple(pltpu.with_memory_space_constraint(a, pltpu.VMEM) for a in arrays)


def multiply_own(plan, left, mine, theirs, after):
    return pl.pallas_call(
        own_kernel,
        out_shape=(pltpu.VMEM(EARLY, jnp.float32), pltpu.SMEM((8,), jnp.int32)),
        in_specs=[SMEM] + [VMEM] * 10 + [ANY] * 2,
        out_specs=(VMEM, SMEM),
        scratch_shapes=[LEFT],
        compiler_params=pltpu.CompilerParams(vmem_limit_bytes=LIMIT),
        cost_estimate=pl.CostEstimate(flops=2 * 96 * TILE**3, bytes_accessed=16 << 20, transcendentals=0),
    )(plan, *in_vmem(*left, *mine, *theirs), *after)


def multiply_other(plan, own_left, left, mine, theirs, early, done):
    return pl.pallas_call(
        other_kernel,
        out_shape=(pltpu.VMEM(MERGED, jnp.float32), pltpu.HBM((PANELS, BLK, TILE), jnp.float32)),
        in_specs=[SMEM] + [VMEM] * 17 + [ANY],
        out_specs=(VMEM, VMEM),
        scratch_shapes=[LEFT, LEFT, pltpu.VMEM((BLK, TILE), jnp.float32)],
        compiler_params=pltpu.CompilerParams(vmem_limit_bytes=LIMIT),
        cost_estimate=pl.CostEstimate(flops=2 * 96 * TILE**3, bytes_accessed=16 << 20, transcendentals=0),
    )(plan, *in_vmem(*own_left, *left, *mine, *theirs, early), token(Y2_COST, *left[1:], done))


def scale_kernel(plan, merged, totals, out, factor):
    d = pl.program_id(0)
    pair = plan[END] // 2

    @pl.when(d == 0)
    def _():
        factor[...] = float(PANELS * PANELS * TILE) / (jnp.sum(totals[...], axis=0) + 1e-6)

    def step(n, carry):
        for u in range(GROUP):
            t = n * GROUP + u
            scaling = factor[pl.ds(t, 1), :]
            for half in range(2):
                tile = merged[t, plan[MERGE + (half * 4 + d) * BLK + t]]
                out[pair if half == 0 else 1 - pair, t] = (tile * tile * scaling).astype(jnp.bfloat16)
        return carry

    lax.fori_loop(0, BLK // GROUP, step, 0)


def scale(plan, merged, totals):
    def place(d, plan):
        away = jnp.where(d == 1, 3, jnp.where(d == 2, 1, jnp.where(d == 3, 2, 0)))
        return (plan[END + 2] + away) % 4, 0, 0, 0

    return pl.pallas_call(
        scale_kernel,
        out_shape=jax.ShapeDtypeStruct((PANELS, BLK, TILE, TILE), jnp.bfloat16),
        grid_spec=pltpu.PrefetchScalarGridSpec(
            num_scalar_prefetch=1,
            grid=(4,),
            in_specs=[VMEM, VMEM],
            out_specs=pl.BlockSpec((2, BLK, TILE, TILE), place),
            scratch_shapes=[pltpu.VMEM((BLK, TILE), jnp.float32)],
        ),
        compiler_params=pltpu.CompilerParams(vmem_limit_bytes=LIMIT),
        cost_estimate=pl.CostEstimate(flops=2 * 192 * TILE**2, bytes_accessed=20 << 20, transcendentals=0),
    )(plan, *in_vmem(merged), totals)


def exchange(send):
    return (send[0],) + tuple(lax.ppermute(part, "y", way) for part, way in zip(send[1:], (UP, ACROSS, DOWN)))


def on_device(tile_values, tile_rows):
    own = tile_values[0]
    pos = jnp.stack([lax.axis_index(a) for a in ("x", "y", "z", "core")]).astype(jnp.int32)
    inner = lax.ppermute(own, "x", INNER)
    outer = lax.ppermute(own, "x", OUTER)
    rows = lax.all_to_all(jnp.broadcast_to(tile_rows, (PANELS, 1, BLK)), ("z", "core"), 0, 0)
    own_rows = jnp.pad(tile_rows, ((0, 0), (OWN_ROWS, TILE - OWN_ROWS - BLK)))
    asks = jnp.broadcast_to(jnp.pad(rows, ((0, 0), (0, 0), (0, TILE - BLK))).reshape(4, 1, 2, TILE) + own_rows, (4, 4, 2, TILE)).reshape(COLS, 2, TILE)
    req = lax.all_to_all(asks, ("y", "x"), 0, 0)
    own_z, rows_z = lax.optimization_barrier((own, rows))
    below = lax.ppermute(own_z, "z", UP)
    above = lax.ppermute(own_z, "z", DOWN)

    their_own = lax.ppermute(own, "core", SWAP)
    arrived = token(TOKEN_COST, inner, outer, their_own)
    *send1, lists = select_own(pos, req, own, inner, arrived)
    left1 = exchange(send1)
    diag = lax.ppermute(outer, "x", INNER)

    far = lax.ppermute(jnp.where(lax.axis_index("core") == 0, below, above), ("z", "core"), FAR)
    plan = make_plan(pos, rows_z, req, diag)
    sent = pltpu.HBM((USED, TILE, TILE), jnp.bfloat16)
    their_own, brought = bring(their_own, send1[0])
    after = (brought, token(DIAG_COST, diag), lists)
    send2 = select(select_other_kernel, (sent,) * 4, lists, (outer, diag), after)
    left2 = exchange(send2)
    mine = (own, below, above)
    kept, *later = lax.optimization_barrier((send2[0], below, above))
    theirs = (their_own, *(lax.ppermute(block, "core", SWAP) for block in later))
    left2 = (kept, *left2[1:])
    early, done = multiply_own(plan, left1, mine, theirs, (kept, token(Y1_LATE_COST, *left1[1:])))
    kept2, far = lax.optimization_barrier((kept, far))
    left2 = (kept2, *left2[1:])
    mine, theirs = (*mine, far), (*theirs, lax.ppermute(far, "core", SWAP))
    merged, totals = multiply_other(plan, left1, left2, mine, theirs, early, done)
    totals = lax.all_to_all(totals, ("z", "core"), 0, 0)
    return scale(plan, merged, totals)[None]


def solution(mesh):
    fine = Mesh(np.asarray(mesh.devices).reshape(4, 2, 4, 4), ("z", "core", "y", "x"))
    rows, cols = ("z", "core"), ("y", "x")
    return jax.shard_map(
        on_device,
        mesh=fine,
        in_specs=(P(rows, cols, None, None), P(rows, cols)),
        out_specs=P(rows, None, cols, None, None),
        check_vma=False,
    )
```
